256 devices in a mesh: replica: 16 (over z_hi, y, core), fsdp: 16 (over x, z_lo).
Axes of the slice: x: 4, y: 4, z: 8 (z_hi: 2, z_lo: 4; z = z_hi * 4 + z_lo), core: 2. Of those that a mesh axis runs over, the one named last changes fastest.
Arguments:
- tokens: bfloat16 [65536, 8192], P(('replica', 'fsdp')), may hold values from -6 to 6
- hidden_grad: bfloat16 [65536, 448], P(('replica', 'fsdp')), may hold values from -6 to 6
- gate_next: bfloat16 [16, 448, 8192], P('replica', None, 'fsdp'), may hold values from -0.0625 to 0.0625
- up_next: bfloat16 [16, 448, 8192], P('replica', None, 'fsdp'), may hold values from -0.0625 to 0.0625
- inner_gate: bfloat16 [16, 448, 8192], P('replica', None, 'fsdp'), may hold values from -10 to 10
- anchor: float32 [448, 8192], P(None, 'fsdp'), may hold values from -2 to 2
- momentum: float32 [448, 8192], P(None, 'fsdp'), may hold values from -4 to 4
Outputs:
- token_grad: bfloat16 [65536, 8192], P(('replica', 'fsdp'))
- gate_grad: bfloat16 [16, 448, 8192], P('replica', None, 'fsdp')
- up_grad: bfloat16 [16, 448, 8192], P('replica', None, 'fsdp')
- new_anchor: float32 [448, 8192], P(None, 'fsdp')
- new_momentum: float32 [448, 8192], P(None, 'fsdp')
The draws below stay inside these ranges and needn't reach their ends.
All inputs are finite; a program needn't handle non-finite values. Where the reference program divides by a largest or mean magnitude, that divisor is 1e-20 or more.
Results may differ from the reference program's by a relative error of at most 0.023.
Values may be sent and summed in bfloat16 or wider, within the bound.
A program may use at most 128 MiB of HBM per device.

```python
import math
import jax
import jax.numpy as jnp
from jax import lax

D = 8192
BLOCK = 128
TOK_DEV = 256
FF_TP = 448
REPLICAS = 16
TOKENS = 65536
N_REPLICA = 16
N_FSDP = 16


def outer_pieces(key):
    key_level = jax.random.fold_in(key, 11)
    key_frac = jax.random.fold_in(key, 12)
    key_scale = jax.random.fold_in(key, 13)
    key_peak = jax.random.fold_in(key, 14)
    key_sign = jax.random.fold_in(key, 15)
    key_base = jax.random.fold_in(key, 16)
    runs = D // BLOCK
    level = jax.random.randint(key_level, (REPLICAS, FF_TP, runs, BLOCK), -7, 8).astype(jnp.float32)
    frac = jax.random.uniform(key_frac, (REPLICAS, FF_TP, runs, BLOCK), jnp.float32, -0.3, 0.3)
    spread = jax.random.uniform(key_scale, (REPLICAS, FF_TP, runs, 1), jnp.float32, math.log(2.0), math.log(8.0))
    scale = jnp.exp(spread)
    peak = jax.random.randint(key_peak, (REPLICAS, FF_TP, runs, 1), 0, BLOCK)
    sign = 2.0 * jax.random.randint(key_sign, (REPLICAS, FF_TP, runs, 1), 0, 2).astype(jnp.float32) - 1.0
    place = jnp.arange(BLOCK, dtype=jnp.int32)[None, None, None, :]
    is_peak = place == peak
    level = jnp.where(is_peak, 7.0 * sign, level)
    frac = jnp.where(is_peak, 0.0, frac)
    frac = jnp.where(level >= 7.0, -jnp.abs(frac), frac)
    frac = jnp.where(level <= -7.0, jnp.abs(frac), frac)
    delta = (scale * (level + frac) / 7.0).reshape(REPLICAS, FF_TP, D)
    base = jnp.clip(0.7 * jax.random.normal(key_base, (FF_TP, D), jnp.float32), -2.0, 2.0)
    return (base, delta)


def draw_anchor(key, part):
    base, delta = outer_pieces(key)
    return base.astype(jnp.float32)


def draw_inner_gate(key, part):
    base, delta = outer_pieces(key)
    return (base[None] - delta).astype(jnp.bfloat16)


def shard_levels(stream_key, extent, shards, least, top_value):
    gain = 1.0
    for dim, blocks in shards:
        draws = jax.random.uniform(jax.random.fold_in(jax.random.fold_in(stream_key, 6), dim), (blocks,), jnp.float32, least / len(shards), top_value / len(shards))
        gain = gain * jnp.repeat(jnp.exp(draws), extent[dim] // blocks).reshape((-1,) + (1,) * (len(extent) - 1 - dim))
    return gain


def centred(own_key, dims, deviation, most, shards=(), kind=jnp.bfloat16):
    array = jax.random.normal(own_key, dims, jnp.float32) * deviation
    if len(shards) > 0:
        array = shard_levels(own_key, dims, shards, -0.22, 0.18) * array
    return jnp.clip(array, min=-most, max=most).astype(kind)


def setup_inputs(seed: int = 0) -> dict:
    keys = jax.random.split(jax.random.key(seed), 8)
    tokens = centred(keys[0], (TOKENS, D), 1.0, 6.0, ((0, 256),))
    hidden_grad = centred(keys[1], (TOKENS, FF_TP), 1.0, 6.0, ((0, 256),))
    gate_next = centred(keys[2], (REPLICAS, FF_TP, D), D ** -0.5, 0.0625, ((0, 16), (2, 16)))
    up_next = centred(keys[3], (REPLICAS, FF_TP, D), D ** -0.5, 0.0625, ((0, 16), (2, 16)))
    inner_gate = draw_inner_gate(jax.random.fold_in(keys[7], 71), 0)
    anchor = draw_anchor(jax.random.fold_in(keys[7], 71), 0)
    momentum = centred(keys[6], (FF_TP, D), 0.5, 4.0, ((1, 16),), jnp.float32)
    return {"tokens": tokens, "hidden_grad": hidden_grad, "gate_next": gate_next, "up_next": up_next, "inner_gate": inner_gate, "anchor": anchor, "momentum": momentum}


eps_scale = 1e-6
outer_mu = 0.9
outer_rate = 0.7


def rounded_sum(cot_rows, token_rows):
    cot_parts = cot_rows.reshape(N_FSDP, TOK_DEV, cot_rows.shape[1])
    token_parts = token_rows.reshape(N_FSDP, TOK_DEV, token_rows.shape[1])

    def add_term(total, pair):
        term = jnp.dot(pair[0].T, pair[1], preferred_element_type=jnp.float32).astype(jnp.bfloat16)
        term = lax.optimization_barrier(term)
        return total + term.astype(jnp.float32), None

    start = jnp.zeros((cot_rows.shape[1], token_rows.shape[1]), jnp.float32)
    total, unused = lax.scan(add_term, start, (cot_parts, token_parts))
    return total.astype(jnp.bfloat16)


def decode_delta(anchor, inner):
    delta = anchor - inner.astype(jnp.float32)
    blocks = delta.reshape(delta.shape[0], delta.shape[1] // BLOCK, BLOCK)
    scale = jnp.max(jnp.abs(blocks), axis=-1, keepdims=True) + eps_scale
    code = jnp.floor((blocks / scale) * 7.0 + 0.5).astype(jnp.bfloat16)
    code = lax.optimization_barrier(code)
    return (scale * code.astype(jnp.float32) / 7.0).reshape(delta.shape)


def reference(tokens, hidden_grad, gate_next, up_next, inner_gate, anchor, momentum):
    rows = N_FSDP * TOK_DEV
    token_parts = []
    gate_parts = []
    up_parts = []
    decoded_total = jnp.zeros(anchor.shape, jnp.float32)
    for rank in range(N_REPLICA):
        inputs = tokens[rank * rows:(rank + 1) * rows]
        cotan = hidden_grad[rank * rows:(rank + 1) * rows].astype(jnp.float32)
        gate = jnp.dot(inputs, gate_next[rank].T, preferred_element_type=jnp.float32)
        upval = jnp.dot(inputs, up_next[rank].T, preferred_element_type=jnp.float32)
        sig = jax.nn.sigmoid(gate)
        gate_cot = (cotan * upval * sig * (1.0 + gate * (1.0 - sig))).astype(jnp.bfloat16)
        up_cot = (cotan * gate * sig).astype(jnp.bfloat16)
        back = jnp.dot(gate_cot, gate_next[rank], preferred_element_type=jnp.float32)
        back = back + jnp.dot(up_cot, up_next[rank], preferred_element_type=jnp.float32)
        token_parts.append(back.astype(jnp.bfloat16))
        gate_parts.append(rounded_sum(gate_cot, inputs))
        up_parts.append(rounded_sum(up_cot, inputs))
        decoded_total = decoded_total + decode_delta(anchor, inner_gate[rank])
    outer_grad = decoded_total / N_REPLICA
    new_momentum = outer_mu * momentum + outer_grad
    new_anchor = anchor - outer_rate * (outer_grad + outer_mu * new_momentum)
    return (jnp.concatenate(token_parts, 0), jnp.stack(gate_parts), jnp.stack(up_parts), new_anchor, new_momentum)
```

```python
import functools
import jax
import jax.numpy as jnp
from jax import lax
from jax.experimental import pallas as pl
from jax.experimental.pallas import tpu as pltpu
from jax.sharding import PartitionSpec as P

MESH = pl.DeviceIdType.MESH
BF16 = jnp.bfloat16
F32 = jnp.float32

EPS = 1e-06
MU = 0.9
RATE = 0.7

T = 256
FF = 448
COLS = 512
QUART = 2048
D = 8192
RUN = 128

BLOCKS = ((0, 128), (128, 128), (256, 128), (384, 64))
GROUPS = ((0, 256), (256, 512), (512, 768), (768, 896))
ROWS = 896
NG = len(GROUPS)
YROWS = 224
YCOLS = 128


def dot_nt(a, b):
    return lax.dot_general(a, b, (((1,), (1,)), ((), ())), preferred_element_type=F32)


def dot_nn(a, b):
    return lax.dot_general(a, b, (((1,), (0,)), ((), ())), preferred_element_type=F32)


def cots(gate, upval, cotan):
    sig = jax.nn.sigmoid(gate)
    gate_cot = cotan * upval * sig * (1.0 + gate * (1.0 - sig))
    up_cot = cotan * gate * sig
    return gate_cot, up_cot


def kernel(
    tokens, hgrad, gate_n, up_n, inner, anchor, momentum,
    tg_out, gg_out, ug_out, na_out, nm_out,
    xq, w, pst, pown, prx, c, ct, tgs, rsi, rso, fin, hg,
    inn, anc, mom, dec, yrx, ysum, zrx, tot,
    w_l, in_l, out_l, tok_s, tok_r, w_s, w_r, p_s, p_r, c_s, c_r, t_s, t_r, g_s, g_r,
    y_s, y_r, zh_s, zh_r, b_s, b_r,
):
    r = lax.axis_index("replica")
    f = lax.axis_index("fsdp")
    x, z = f // 4, f % 4
    zh, y, core = r // 8, (r // 2) % 4, r % 2
    low = z < 2
    end = (z == 0) | (z == 3)
    mid = (z == 1) | (z == 2)
    step = jnp.where(low, 1, -1)
    inward = (r, f + step)
    outward = (r, f - step)

    def xdev(k):
        return (r, ((x + k) % 4) * 4 + z)

    def ydev(dy, dc):
        return (zh * 8 + ((y + dy) % 4) * 2 + (core + dc) % 2, f)

    zpart = ((r + 8) % 16, f)
    ypeers = [(dy, dc) for dy in range(4) for dc in range(2) if (dy, dc) != (0, 0)]

    def colsz(zz):
        return pl.ds(pl.multiple_of(zz * COLS, COLS), COLS)

    def quart(xx):
        return pl.ds(pl.multiple_of(xx * QUART, QUART), QUART)

    w_local = []
    for b, (u0, n) in enumerate(BLOCKS):
        at = 2 * u0
        w_local.append(pltpu.make_async_copy(
            gate_n.at[0, pl.ds(u0, n)], w.at[pl.ds(at, n), colsz(z)], w_l.at[2 * b]))
        w_local.append(pltpu.make_async_copy(
            up_n.at[0, pl.ds(u0, n)], w.at[pl.ds(at + n, n), colsz(z)], w_l.at[2 * b + 1]))
    for q in w_local:
        q.start()
    own_tok = pltpu.make_async_copy(tokens.at[:, quart(x)], xq.at[0], in_l.at[0])
    in_inner = pltpu.make_async_copy(inner.at[0], inn, in_l.at[1])
    in_anchor = pltpu.make_async_copy(anchor, anc, in_l.at[2])
    in_mom = pltpu.make_async_copy(momentum, mom, in_l.at[3])
    in_hg = pltpu.make_async_copy(hgrad, hg, in_l.at[4])
    for q in (own_tok, in_inner, in_anchor, in_mom, in_hg):
        q.start()

    barrier = pltpu.get_barrier_semaphore()

    def greet(dev):
        pl.semaphore_signal(barrier, inc=1, device_id=dev, device_id_type=MESH)

    for k in (1, 2, 3):
        greet(xdev(k))
    greet(inward)

    @pl.when(mid)
    def _():
        greet(outward)

    for dy, dc in ypeers:
        greet(ydev(dy, dc))
    greet(zpart)
    pl.semaphore_wait(barrier, 12 + jnp.where(mid, 1, 0))

    def remote(src, dst, ss, rs, dev):
        return pltpu.make_async_remote_copy(
            src_ref=src, dst_ref=dst, send_sem=ss, recv_sem=rs, device_id=dev, device_id_type=MESH)

    tok = {k: remote(tokens.at[:, quart((x + k) % 4)], xq.at[k], tok_s.at[k], tok_r.at[k], xdev(k))
           for k in (1, 3, 2)}
    for k in (1, 3, 2):
        tok[k].start()

    near_end = jnp.where(low, 0, 3)
    far_mid = jnp.where(low, 2, 1)
    far_end = jnp.where(low, 3, 0)

    def wpiece(g, origin, slot, dev):
        a, b = GROUPS[g]
        ref = w.at[pl.ds(a, b - a), colsz(origin)]
        return remote(ref, ref, w_s.at[g, slot], w_r.at[g, origin], dev)

    def w_own(g):
        wpiece(g, z, 0, inward).start()

        @pl.when(mid)
        def _():
            wpiece(g, z, 1, outward).start()

    def w_wait_local(g):
        w_local[2 * g].wait()
        w_local[2 * g + 1].wait()

    def w_forward(g):
        @pl.when(mid)
        def _():
            wpiece(g, near_end, 2, inward).wait_recv()
            wpiece(g, near_end, 2, inward).start()
            wpiece(g, far_mid, 3, outward).wait_recv()
            wpiece(g, far_mid, 3, outward).start()

        if g + 1 < NG:
            w_wait_local(g + 1)
            w_own(g + 1)

        @pl.when(mid)
        def _():
            wpiece(g, far_end, 4, outward).wait_recv()
            wpiece(g, far_end, 4, outward).start()

        @pl.when(end)
        def _():
            wpiece(g, z + step, 0, inward).wait_recv()
            wpiece(g, far_mid, 0, inward).wait_recv()
            wpiece(g, far_end, 0, inward).wait_recv()

    def w_drain(g):
        wpiece(g, z, 0, inward).wait_send()

        @pl.when(mid)
        def _():
            wpiece(g, z, 1, outward).wait_send()
            wpiece(g, near_end, 2, inward).wait_send()
            wpiece(g, far_mid, 3, outward).wait_send()
            wpiece(g, far_end, 4, outward).wait_send()

    def yslice(ref, yy, cc):
        return ref.at[pl.ds(pl.multiple_of(cc * YROWS, YROWS), YROWS),
                      pl.ds(pl.multiple_of(yy * YCOLS, YCOLS), YCOLS)]

    def yscatter(i):
        dy, dc = ypeers[i]
        slot = dy * 2 + dc
        return remote(yslice(dec, (y + dy) % 4, (core + dc) % 2), yrx.at[slot],
                      y_s.at[slot], y_r.at[slot], ydev(dy, dc))

    def ygather(i):
        dy, dc = ypeers[i]
        slot = dy * 2 + dc
        return remote(yslice(tot, y, core), yslice(tot, y, core), b_s.at[slot], b_r.at[slot], ydev(dy, dc))

    def ygather_in(i):
        dy, dc = ypeers[i]
        slot = dy * 2 + dc
        ref = yslice(tot, (y + 4 - dy) % 4, (core + dc) % 2)
        return remote(ref, ref, b_s.at[slot], b_r.at[slot], ydev(dy, dc))

    zswap = remote(ysum.at[...], zrx.at[...], zh_s.at[0], zh_r.at[0], zpart)

    def outer_decode():
        in_anchor.wait()
        in_inner.wait()
        for j in range(COLS // RUN):
            s = slice(j * RUN, (j + 1) * RUN)
            delta = anc[:, s] - inn[:, s].astype(F32)
            scale = jnp.max(jnp.abs(delta), axis=-1, keepdims=True) + EPS
            code = jnp.floor((delta / scale) * 7.0 + 0.5)
            dec[:, s] = (scale * code / 7.0).astype(BF16)
        for i in range(7):
            yscatter(i).start()

    def outer_sum():
        total = yslice(dec, y, core)[...].astype(F32)
        for i in range(7):
            yscatter(i).wait_recv()
        for i in range(7):
            dy, dc = ypeers[i]
            total = total + yrx[dy * 2 + dc].astype(F32)
        ysum[...] = total
        zswap.start()

    def outer_share():
        zswap.wait_recv()
        yslice(tot, y, core)[...] = ysum[...] + zrx[...]
        for i in range(7):
            ygather(i).start()

    out_na = pltpu.make_async_copy(anc, na_out, out_l.at[0])
    out_nm = pltpu.make_async_copy(mom, nm_out, out_l.at[1])

    def outer_finish():
        in_mom.wait()
        for i in range(7):
            ygather_in(i).wait_recv()
        grad = tot[...] / 16.0
        new_m = MU * mom[...] + grad
        mom[...] = new_m
        anc[...] = anc[...] - RATE * (grad + MU * new_m)
        out_na.start()
        out_nm.start()

    def lanes(g):
        a, b = GROUPS[g]
        return pl.ds(a, b - a)

    def part_copy(g, k):
        return remote(pst.at[k, :, lanes(g)], prx.at[k, :, lanes(g)], p_s.at[g, k], p_r.at[g, k], xdev(4 - k))

    def cot_copy(g, k):
        return remote(c.at[0, :, lanes(g)], c.at[k, :, lanes(g)], c_s.at[g, k], c_r.at[g, k], xdev(k))

    def partials(g):
        a, b = GROUPS[g]
        for k in (2, 1, 3):
            pst[k, :, a:b] = dot_nt(xq[k], w[a:b, :]).astype(BF16)
            part_copy(g, k).start()
        pown[:, a:b] = dot_nt(xq[0], w[a:b, :])

    def owner(g):
        a, b = GROUPS[g]
        for k in (1, 3, 2):
            part_copy(g, k).wait_recv()
        for u0, n in BLOCKS:
            at = 2 * u0
            if not a <= at < b:
                continue
            full = slice(at, at + 2 * n)
            total = pown[:, full]
            for k in (1, 2, 3):
                total = total + prx[k, :, full].astype(F32)
            if n == 128:
                gc, uc = cots(total[:, :n], total[:, n:], hg[:, u0:u0 + n].astype(F32))
                c[0, :, at:at + n] = gc.astype(BF16)
                c[0, :, at + n:at + 2 * n] = uc.astype(BF16)
            else:
                half = hg[:, u0:u0 + n].astype(F32)
                cotan = jnp.concatenate([half, half], axis=1)
                turned = pltpu.roll(total, n, 1)
                first = lax.broadcasted_iota(jnp.int32, total.shape, 1) < n
                gc, uc = cots(jnp.where(first, total, turned), jnp.where(first, turned, total), cotan)
                c[0, :, full] = jnp.where(first, gc, uc).astype(BF16)
        for k in (2, 1, 3):
            cot_copy(g, k).start()

    def gathered(g):
        a, b = GROUPS[g]
        for k in (1, 3, 2):
            cot_copy(g, k).wait_recv()
        for k in range(4):
            ct[a:b, k * T:(k + 1) * T] = c[k, :, a:b].T

    dest_a = jnp.where(low, 3, 0)
    dest_b = jnp.where(low, 2, 1)
    dest_c = jnp.where(z == 0, 1, jnp.where(z == 1, 0, jnp.where(z == 2, 3, 2)))
    dev_c = (r, f + jnp.where(end, step, -step))
    slot_a = jnp.where(end, 0, 3)
    slot_b = jnp.where(end, 1, 4)
    sends = ((dest_a, inward, slot_a, 0), (dest_b, inward, slot_b, 1), (dest_c, dev_c, 2, 3))

    def grad_copy(g, i):
        a, b = GROUPS[g]
        dest, dev, slot, _ = sends[i]
        return remote(rso.at[i, pl.ds(a, b - a)], rsi.at[slot, pl.ds(a, b - a)],
                      g_s.at[g, i], g_r.at[g, slot], dev)

    def grad_in(g, slot):
        a, b = GROUPS[g]
        ref = rsi.at[slot, pl.ds(a, b - a)]
        return remote(ref, ref, g_s.at[g, 0], g_r.at[g, slot], inward)

    def grad_term(g, dest):
        a, b = GROUPS[g]
        return dot_nn(ct[a:b, :], xq[:, :, colsz(dest)].reshape(4 * T, COLS))

    def grad_send(g, i):
        a, b = GROUPS[g]
        dest, _, _, arrives = sends[i]
        rso[i, a:b] = grad_term(g, dest).astype(BF16)

        @pl.when(mid)
        def _():
            grad_in(g, arrives).wait_recv()
            rso[i, a:b] = (rso[i, a:b].astype(F32) + rsi[arrives, a:b].astype(F32)).astype(BF16)

        grad_copy(g, i).start()

    def grad_own(g):
        a, b = GROUPS[g]
        pown2 = grad_term(g, z)
        grad_in(g, 2).wait_recv()
        pown2 = pown2 + rsi[2, a:b].astype(F32)

        @pl.when(mid)
        def _():
            grad_in(g, 4).wait_recv()
            fin[a:b] = (pown2 + rsi[4, a:b].astype(F32)).astype(BF16)

        @pl.when(end)
        def _():
            fin[a:b] = pown2.astype(BF16)

        for i in out_blocks(g):
            fin_out[i].start()

    fin_out = []
    for b, (u0, n) in enumerate(BLOCKS):
        at = 2 * u0
        fin_out.append(pltpu.make_async_copy(
            fin.at[pl.ds(at, n)], gg_out.at[0, pl.ds(u0, n)], out_l.at[3 + 2 * b]))
        fin_out.append(pltpu.make_async_copy(
            fin.at[pl.ds(at + n, n)], ug_out.at[0, pl.ds(u0, n)], out_l.at[4 + 2 * b]))

    def out_blocks(g):
        return (2 * g, 2 * g + 1)

    def tg_copy(k):
        return remote(tgs.at[k], tg_out.at[:, quart(x)], t_s.at[k], t_r.at[k], xdev(4 - k))

    tg_own = pltpu.make_async_copy(tgs.at[0], tg_out.at[:, quart(x)], out_l.at[2])

    def tg_in(k):
        ref = tg_out.at[:, quart((x + k) % 4)]
        return remote(tgs.at[k], ref, t_s.at[k], t_r.at[k], xdev(4 - k))

    def token_grad(k):
        for j in range(4):
            s = slice(j * COLS, (j + 1) * COLS)
            tgs[k, :, s] = dot_nn(c[k], w[:, s]).astype(BF16)
        if k:
            tg_copy(k).start()
        else:
            tg_own.start()

    w_wait_local(0)
    w_own(0)
    outer_decode()
    w_forward(0)
    outer_sum()
    w_forward(1)
    outer_share()
    own_tok.wait()
    in_hg.wait()
    for k in (1, 3, 2):
        tok[k].wait_recv()
    partials(0)
    partials(1)
    w_forward(2)
    partials(2)
    owner(0)
    w_forward(3)
    partials(3)
    owner(1)
    gathered(0)
    for i in range(3):
        @pl.when(end)
        def _():
            grad_send(0, i)
    owner(2)
    owner(3)
    gathered(1)
    for i in range(3):
        @pl.when(end)
        def _():
            grad_send(1, i)
    gathered(2)
    gathered(3)
    for k in (2, 1, 3):
        token_grad(k)
    for g in range(2):
        for i in range(3):
            @pl.when(mid)
            def _():
                grad_send(g, i)
    for i in range(3):
        grad_send(2, i)
    for i in range(3):
        grad_send(3, i)
    token_grad(0)
    outer_finish()
    for g in range(4):
        grad_own(g)

    for k in (1, 3, 2):
        tg_in(k).wait_recv()
    for k in (1, 2, 3):
        tok[k].wait_send()
        tg_copy(k).wait_send()
        for g in range(NG):
            part_copy(g, k).wait_send()
            cot_copy(g, k).wait_send()
    for g in range(NG):
        w_drain(g)
        for i in range(3):
            grad_copy(g, i).wait_send()
    for i in range(7):
        yscatter(i).wait_send()
        ygather(i).wait_send()
    zswap.wait_send()
    tg_own.wait()
    out_na.wait()
    out_nm.wait()
    for q in fin_out:
        q.wait()


def shards(tokens, hidden_grad, gate_next, up_next, inner_gate, anchor, momentum):
    dma = pltpu.SemaphoreType.DMA
    return pl.pallas_call(
        kernel,
        out_shape=(
            jax.ShapeDtypeStruct((T, D), BF16),
            jax.ShapeDtypeStruct((1, FF, COLS), BF16),
            jax.ShapeDtypeStruct((1, FF, COLS), BF16),
            jax.ShapeDtypeStruct((FF, COLS), F32),
            jax.ShapeDtypeStruct((FF, COLS), F32),
        ),
        in_specs=[pl.BlockSpec(memory_space=pl.ANY)] * 7,
        out_specs=[pl.BlockSpec(memory_space=pl.ANY)] * 5,
        scratch_shapes=[
            pltpu.VMEM((4, T, QUART), BF16),
            pltpu.VMEM((ROWS, QUART), BF16),
            pltpu.VMEM((4, T, ROWS), BF16),
            pltpu.VMEM((T, ROWS), F32),
            pltpu.VMEM((4, T, ROWS), BF16),
            pltpu.VMEM((4, T, ROWS), BF16),
            pltpu.VMEM((ROWS, 4 * T), BF16),
            pltpu.VMEM((4, T, QUART), BF16),
            pltpu.VMEM((5, ROWS, COLS), BF16),
            pltpu.VMEM((3, ROWS, COLS), BF16),
            pltpu.VMEM((ROWS, COLS), BF16),
            pltpu.VMEM((T, FF), BF16),
            pltpu.VMEM((FF, COLS), BF16),
            pltpu.VMEM((FF, COLS), F32),
            pltpu.VMEM((FF, COLS), F32),
            pltpu.VMEM((FF, COLS), BF16),
            pltpu.VMEM((8, YROWS, YCOLS), BF16),
            pltpu.VMEM((YROWS, YCOLS), F32),
            pltpu.VMEM((YROWS, YCOLS), F32),
            pltpu.VMEM((FF, COLS), F32),
            dma((8,)),
            dma((5,)),
            dma((11,)),
            dma((4,)), dma((4,)),
            dma((NG, 5)), dma((NG, 4)),
            dma((NG, 4)), dma((NG, 4)),
            dma((NG, 4)), dma((NG, 4)),
            dma((4,)), dma((4,)),
            dma((NG, 3)), dma((NG, 5)),
            dma((8,)), dma((8,)),
            dma((1,)), dma((1,)),
            dma((8,)), dma((8,)),
        ],
        compiler_params=pltpu.CompilerParams(
            collective_id=0, has_side_effects=True, vmem_limit_bytes=60 * 1024 * 1024
        ),
        cost_estimate=pl.CostEstimate(
            flops=11_300_000_000, bytes_accessed=16_000_000, transcendentals=T * FF
        ),
    )(tokens, hidden_grad, gate_next, up_next, inner_gate, anchor, momentum)


def solution(mesh):
    return jax.shard_map(
        shards,
        mesh=mesh,
        in_specs=(
            P(("replica", "fsdp"), None),
            P(("replica", "fsdp"), None),
            P("replica", None, "fsdp"),
            P("replica", None, "fsdp"),
            P("replica", None, "fsdp"),
            P(None, "fsdp"),
            P(None, "fsdp"),
        ),
        out_specs=(
            P(("replica", "fsdp"), None),
            P("replica", None, "fsdp"),
            P("replica", None, "fsdp"),
            P(None, "fsdp"),
            P(None, "fsdp"),
        ),
        check_vma=False,
    )
```

```python
import functools
import jax
import jax.numpy as jnp
from jax import lax
from jax.experimental import pallas as pl
from jax.experimental.pallas import tpu as pltpu
from jax.sharding import PartitionSpec as P

MESH = pl.DeviceIdType.MESH
BF16 = jnp.bfloat16
F32 = jnp.float32

EPS = 1e-06
MU = 0.9
RATE = 0.7

T = 256
FF = 448
COLS = 512
QUART = 2048
D = 8192
RUN = 128

BLOCKS = ((0, 128), (128, 128), (256, 128), (384, 64))
GROUPS = ((0, 256), (256, 512), (512, 768), (768, 896))
ROWS = 896
NG = len(GROUPS)
YROWS = 224
YCOLS = 128
PARTS = 8


def dot_nt(a, b):
    return lax.dot_general(a, b, (((1,), (1,)), ((), ())), preferred_element_type=F32)


def dot_nn(a, b):
    return lax.dot_general(a, b, (((1,), (0,)), ((), ())), preferred_element_type=F32)


def cots(gate, upval, cotan):
    sig = jax.nn.sigmoid(gate)
    gate_cot = cotan * upval * sig * (1.0 + gate * (1.0 - sig))
    up_cot = cotan * gate * sig
    return gate_cot, up_cot


def kernel(
    tokens, hgrad, gate_n, up_n, inner, anchor, momentum,
    tg_out, gg_out, ug_out, na_out, nm_out,
    xq, w, pst, pown, prx, c, ct, tgs, rsi, rso, fin, hgt, hg,
    inn, anc, mom, dec, yrx, ysum, zrx, tot,
    w_l, in_l, out_l, tok_s, tok_r, w_s, w_r, p_s, p_r, c_s, c_r, t_s, t_r, g_s, g_r,
    y_s, y_r, zh_s, zh_r, b_s, b_r,
):
    r = lax.axis_index("replica")
    f = lax.axis_index("fsdp")
    x, z = f // 4, f % 4
    zh, y, core = r // 8, (r // 2) % 4, r % 2
    low = z < 2
    end = (z == 0) | (z == 3)
    mid = (z == 1) | (z == 2)
    step = jnp.where(low, 1, -1)
    inward = (r, f + step)
    outward = (r, f - step)

    def xdev(k):
        return (r, ((x + k) % 4) * 4 + z)

    def ydev(dy, dc):
        return (zh * 8 + ((y + dy) % 4) * 2 + (core + dc) % 2, f)

    zpart = ((r + 8) % 16, f)
    ypeers = [(dy, dc) for dy in range(4) for dc in range(2) if (dy, dc) != (0, 0)]

    def colsz(zz):
        return pl.ds(pl.multiple_of(zz * COLS, COLS), COLS)

    def quart(xx):
        return pl.ds(pl.multiple_of(xx * QUART, QUART), QUART)

    w_local = []
    for b, (u0, n) in enumerate(BLOCKS):
        at = 2 * u0
        w_local.append(pltpu.make_async_copy(
            gate_n.at[0, pl.ds(u0, n)], w.at[pl.ds(at, n), colsz(z)], w_l.at[2 * b]))
        w_local.append(pltpu.make_async_copy(
            up_n.at[0, pl.ds(u0, n)], w.at[pl.ds(at + n, n), colsz(z)], w_l.at[2 * b + 1]))
    for q in w_local:
        q.start()
    own_tok = pltpu.make_async_copy(tokens.at[:, quart(x)], xq.at[0], in_l.at[0])
    in_inner = pltpu.make_async_copy(inner.at[0], inn, in_l.at[1])
    in_anchor = pltpu.make_async_copy(anchor, anc, in_l.at[2])
    in_mom = pltpu.make_async_copy(momentum, mom, in_l.at[3])
    in_hg = pltpu.make_async_copy(hgrad, hgt, in_l.at[4])
    for q in (own_tok, in_inner, in_anchor, in_mom, in_hg):
        q.start()

    barrier = pltpu.get_barrier_semaphore()

    def greet(dev):
        pl.semaphore_signal(barrier, inc=1, device_id=dev, device_id_type=MESH)

    for k in (1, 2, 3):
        greet(xdev(k))
    greet(inward)

    @pl.when(mid)
    def _():
        greet(outward)

    for dy, dc in ypeers:
        greet(ydev(dy, dc))
    greet(zpart)
    pl.semaphore_wait(barrier, 12 + jnp.where(mid, 1, 0))

    def remote(src, dst, ss, rs, dev):
        return pltpu.make_async_remote_copy(
            src_ref=src, dst_ref=dst, send_sem=ss, recv_sem=rs, device_id=dev, device_id_type=MESH)

    tok = {k: remote(tokens.at[:, quart((x + k) % 4)], xq.at[k], tok_s.at[k], tok_r.at[k], xdev(k))
           for k in (1, 3, 2)}
    for k in (1, 3, 2):
        tok[k].start()

    near_end = jnp.where(low, 0, 3)
    far_mid = jnp.where(low, 2, 1)
    far_end = jnp.where(low, 3, 0)

    def wpiece(g, origin, slot, dev):
        a, b = GROUPS[g]
        ref = w.at[pl.ds(a, b - a), colsz(origin)]
        return remote(ref, ref, w_s.at[g, slot], w_r.at[g, origin], dev)

    def w_own(g):
        wpiece(g, z, 0, inward).start()

        @pl.when(mid)
        def _():
            wpiece(g, z, 1, outward).start()

    def w_wait_local(g):
        w_local[2 * g].wait()
        w_local[2 * g + 1].wait()

    def w_near(g):
        @pl.when(mid)
        def _():
            wpiece(g, near_end, 2, inward).wait_recv()
            wpiece(g, near_end, 2, inward).start()
            wpiece(g, far_mid, 3, outward).wait_recv()
            wpiece(g, far_mid, 3, outward).start()

        if g + 1 < NG:
            w_wait_local(g + 1)
            w_own(g + 1)

    def w_far(g):
        @pl.when(mid)
        def _():
            wpiece(g, far_end, 4, outward).wait_recv()
            wpiece(g, far_end, 4, outward).start()

        @pl.when(end)
        def _():
            wpiece(g, z + step, 0, inward).wait_recv()
            wpiece(g, far_mid, 0, inward).wait_recv()
            wpiece(g, far_end, 0, inward).wait_recv()

    def w_drain(g):
        wpiece(g, z, 0, inward).wait_send()

        @pl.when(mid)
        def _():
            wpiece(g, z, 1, outward).wait_send()
            wpiece(g, near_end, 2, inward).wait_send()
            wpiece(g, far_mid, 3, outward).wait_send()
            wpiece(g, far_end, 4, outward).wait_send()

    def yslice(ref, yy, cc):
        return ref.at[pl.ds(pl.multiple_of(cc * YROWS, YROWS), YROWS),
                      pl.ds(pl.multiple_of(yy * YCOLS, YCOLS), YCOLS)]

    def yscatter(i):
        dy, dc = ypeers[i]
        slot = dy * 2 + dc
        return remote(yslice(dec, (y + dy) % 4, (core + dc) % 2), yrx.at[slot],
                      y_s.at[slot], y_r.at[slot], ydev(dy, dc))

    def ygather(i):
        dy, dc = ypeers[i]
        slot = dy * 2 + dc
        return remote(yslice(tot, y, core), yslice(tot, y, core), b_s.at[slot], b_r.at[slot], ydev(dy, dc))

    def ygather_in(i):
        dy, dc = ypeers[i]
        slot = dy * 2 + dc
        ref = yslice(tot, (y + 4 - dy) % 4, (core + dc) % 2)
        return remote(ref, ref, b_s.at[slot], b_r.at[slot], ydev(dy, dc))

    zswap = remote(ysum.at[...], zrx.at[...], zh_s.at[0], zh_r.at[0], zpart)

    def outer_decode():
        in_anchor.wait()
        in_inner.wait()
        for j in range(COLS // RUN):
            s = slice(j * RUN, (j + 1) * RUN)
            delta = anc[:, s] - inn[:, s].astype(F32)
            scale = jnp.max(jnp.abs(delta), axis=-1, keepdims=True) + EPS
            code = jnp.floor((delta / scale) * 7.0 + 0.5)
            dec[:, s] = (scale * code / 7.0).astype(BF16)
        for i in range(7):
            yscatter(i).start()

    def outer_sum():
        total = yslice(dec, y, core)[...].astype(F32)
        for i in range(7):
            yscatter(i).wait_recv()
        for i in range(7):
            dy, dc = ypeers[i]
            total = total + yrx[dy * 2 + dc].astype(F32)
        ysum[...] = total
        zswap.start()

    def outer_share():
        zswap.wait_recv()
        yslice(tot, y, core)[...] = ysum[...] + zrx[...]
        for i in range(7):
            ygather(i).start()

    out_na = pltpu.make_async_copy(anc, na_out, out_l.at[0])
    out_nm = pltpu.make_async_copy(mom, nm_out, out_l.at[1])

    def outer_finish():
        in_mom.wait()
        for i in range(7):
            ygather_in(i).wait_recv()
        grad = tot[...] / 16.0
        new_m = MU * mom[...] + grad
        mom[...] = new_m
        anc[...] = anc[...] - RATE * (grad + MU * new_m)
        out_na.start()
        out_nm.start()

    def lanes(g):
        a, b = GROUPS[g]
        return pl.ds(a, b - a)

    def part_copy(g, k):
        return remote(pst.at[k, :, lanes(g)], prx.at[k, :, lanes(g)], p_s.at[g, k], p_r.at[g, k], xdev(4 - k))

    def cot_copy(g, k):
        return remote(c.at[0, :, lanes(g)], c.at[k, :, lanes(g)], c_s.at[g, k], c_r.at[g, k], xdev(k))

    def partials(g, ks):
        a, b = GROUPS[g]
        for k in ks:
            if k:
                pst[k, :, a:b] = dot_nt(xq[k], w[a:b, :]).astype(BF16)
                part_copy(g, k).start()
            else:
                pown[:, a:b] = dot_nt(xq[0], w[a:b, :])

    def owner(g):
        a, b = GROUPS[g]
        for k in (1, 3, 2):
            part_copy(g, k).wait_recv()
        for u0, n in BLOCKS:
            at = 2 * u0
            if not a <= at < b:
                continue
            full = slice(at, at + 2 * n)
            total = pown[:, full]
            for k in (1, 2, 3):
                total = total + prx[k, :, full].astype(F32)
            if n == 128:
                gc, uc = cots(total[:, :n], total[:, n:], hg[:, u0:u0 + n].astype(F32))
                c[0, :, at:at + n] = gc.astype(BF16)
                c[0, :, at + n:at + 2 * n] = uc.astype(BF16)
            else:
                half = hg[:, u0:u0 + n].astype(F32)
                cotan = jnp.concatenate([half, half], axis=1)
                turned = pltpu.roll(total, n, 1)
                first = lax.broadcasted_iota(jnp.int32, total.shape, 1) < n
                gc, uc = cots(jnp.where(first, total, turned), jnp.where(first, turned, total), cotan)
                c[0, :, full] = jnp.where(first, gc, uc).astype(BF16)
        for k in (2, 1, 3):
            cot_copy(g, k).start()

    def gathered(g):
        a, b = GROUPS[g]
        for k in (1, 3, 2):
            cot_copy(g, k).wait_recv()
        for k in range(4):
            ct[a:b, k * T:(k + 1) * T] = c[k, :, a:b].T

    dest_a = jnp.where(low, 3, 0)
    dest_b = jnp.where(low, 2, 1)
    dest_c = jnp.where(z == 0, 1, jnp.where(z == 1, 0, jnp.where(z == 2, 3, 2)))
    dev_c = (r, f + jnp.where(end, step, -step))
    slot_a = jnp.where(end, 0, 3)
    slot_b = jnp.where(end, 1, 4)
    sends = ((dest_a, inward, slot_a, 0), (dest_b, inward, slot_b, 1), (dest_c, dev_c, 2, 3))

    def grad_copy(g, i):
        a, b = GROUPS[g]
        dest, dev, slot, _ = sends[i]
        return remote(rso.at[i, pl.ds(a, b - a)], rsi.at[slot, pl.ds(a, b - a)],
                      g_s.at[g, i], g_r.at[g, slot], dev)

    def grad_in(g, slot):
        a, b = GROUPS[g]
        ref = rsi.at[slot, pl.ds(a, b - a)]
        return remote(ref, ref, g_s.at[g, 0], g_r.at[g, slot], inward)

    def grad_term(g, dest):
        a, b = GROUPS[g]
        return dot_nn(ct[a:b, :], xq[:, :, colsz(dest)].reshape(4 * T, COLS))

    def grad_send(g, i):
        a, b = GROUPS[g]
        dest, _, _, arrives = sends[i]
        rso[i, a:b] = grad_term(g, dest).astype(BF16)

        @pl.when(mid)
        def _():
            grad_in(g, arrives).wait_recv()
            rso[i, a:b] = (rso[i, a:b].astype(F32) + rsi[arrives, a:b].astype(F32)).astype(BF16)

        grad_copy(g, i).start()

    def grad_own(g):
        a, b = GROUPS[g]
        pown2 = grad_term(g, z)
        grad_in(g, 2).wait_recv()
        pown2 = pown2 + rsi[2, a:b].astype(F32)

        @pl.when(mid)
        def _():
            grad_in(g, 4).wait_recv()
            fin[a:b] = (pown2 + rsi[4, a:b].astype(F32)).astype(BF16)

        @pl.when(end)
        def _():
            fin[a:b] = pown2.astype(BF16)

        for i in out_blocks(g):
            fin_out[i].start()

    fin_out = []
    for b, (u0, n) in enumerate(BLOCKS):
        at = 2 * u0
        fin_out.append(pltpu.make_async_copy(
            fin.at[pl.ds(at, n)], gg_out.at[0, pl.ds(u0, n)], out_l.at[3 + 2 * b]))
        fin_out.append(pltpu.make_async_copy(
            fin.at[pl.ds(at + n, n)], ug_out.at[0, pl.ds(u0, n)], out_l.at[4 + 2 * b]))

    def out_blocks(g):
        return (2 * g, 2 * g + 1)

    def tg_cols(xx, h):
        return pl.ds(pl.multiple_of(xx * QUART + h * (QUART // 2), QUART // 2), QUART // 2)

    def tg_copy(k, h):
        return remote(tgs.at[k, :, pl.ds(h * (QUART // 2), QUART // 2)], tg_out.at[:, tg_cols(x, h)],
                      t_s.at[k, h], t_r.at[k, h], xdev(4 - k))

    tg_own = pltpu.make_async_copy(tgs.at[0], tg_out.at[:, quart(x)], out_l.at[2])

    def tg_in(k, h):
        return remote(tgs.at[k, :, pl.ds(h * (QUART // 2), QUART // 2)], tg_out.at[:, tg_cols((x + k) % 4, h)],
                      t_s.at[k, h], t_r.at[k, h], xdev(4 - k))

    def token_grad(k, h):
        for j in (2 * h, 2 * h + 1):
            s = slice(j * COLS, (j + 1) * COLS)
            tgs[k, :, s] = dot_nn(c[k], w[:, s]).astype(BF16)
        if k:
            tg_copy(k, h).start()

    w_wait_local(0)
    w_own(0)
    outer_decode()
    in_hg.wait()
    hg[...] = hgt[...].T
    own_tok.wait()
    w_near(0)
    outer_sum()
    w_far(0)
    w_near(1)
    tok[1].wait_recv()
    tok[3].wait_recv()
    partials(0, (1, 3, 0))
    w_far(1)
    outer_share()
    w_near(2)
    tok[2].wait_recv()
    partials(0, (2,))
    partials(1, (1, 3, 2, 0))
    owner(0)
    w_far(2)
    w_near(3)
    partials(2, (1, 3, 2, 0))
    owner(1)
    w_far(3)
    partials(3, (1, 3, 2, 0))
    gathered(0)
    for i in range(3):
        @pl.when(end)
        def _():
            grad_send(0, i)
    owner(2)
    gathered(1)
    for i in range(3):
        @pl.when(end)
        def _():
            grad_send(1, i)
    owner(3)
    for i in range(2):
        @pl.when(mid)
        def _():
            grad_send(0, i)
    gathered(2)
    gathered(3)
    for h in range(2):
        for k in (2, 1, 3):
            token_grad(k, h)

    @pl.when(mid)
    def _():
        grad_send(0, 2)
    for i in range(3):
        @pl.when(mid)
        def _():
            grad_send(1, i)
    for i in range(3):
        grad_send(2, i)
    for i in range(3):
        grad_send(3, i)
    token_grad(0, 0)
    token_grad(0, 1)
    tg_own.start()
    outer_finish()
    for g in range(4):
        grad_own(g)

    for k in (1, 3, 2):
        for h in range(2):
            tg_in(k, h).wait_recv()
    for k in (1, 2, 3):
        tok[k].wait_send()
        for h in range(2):
            tg_copy(k, h).wait_send()
        for g in range(NG):
            part_copy(g, k).wait_send()
            cot_copy(g, k).wait_send()
    for g in range(NG):
        w_drain(g)
        for i in range(3):
            grad_copy(g, i).wait_send()
    for i in range(7):
        yscatter(i).wait_send()
        ygather(i).wait_send()
    zswap.wait_send()
    tg_own.wait()
    out_na.wait()
    out_nm.wait()
    for q in fin_out:
        q.wait()


def results(tg, gg, ug, na, nm, tg_out, gg_out, ug_out, na_out, nm_out, tv, gv, uv, av, mv, in_s, out_s):
    ways = [(na, av, na_out), (nm, mv, nm_out), (gg, gv, gg_out), (ug, uv, ug_out)]
    for i in range(PARTS):
        rows = pl.ds(i * (T // PARTS), T // PARTS)
        ways.append((tg.at[rows], tv.at[rows], tg_out.at[rows]))
    ins = [pltpu.make_async_copy(src, via, in_s.at[i]) for i, (src, via, _) in enumerate(ways)]
    outs = [pltpu.make_async_copy(via, dst, out_s.at[i]) for i, (_, via, dst) in enumerate(ways)]
    for q in ins:
        q.start()
    for q, o in zip(ins, outs):
        q.wait()
        o.start()
    for o in outs:
        o.wait()


def shards(tokens, hidden_grad, gate_next, up_next, inner_gate, anchor, momentum):
    dma = pltpu.SemaphoreType.DMA
    shapes = (
        jax.ShapeDtypeStruct((T, D), BF16),
        jax.ShapeDtypeStruct((1, FF, COLS), BF16),
        jax.ShapeDtypeStruct((1, FF, COLS), BF16),
        jax.ShapeDtypeStruct((FF, COLS), F32),
        jax.ShapeDtypeStruct((FF, COLS), F32),
    )
    outs = pl.pallas_call(
        kernel,
        out_shape=shapes,
        in_specs=[pl.BlockSpec(memory_space=pl.ANY)] * 7,
        out_specs=[pl.BlockSpec(memory_space=pl.ANY)] * 5,
        scratch_shapes=[
            pltpu.VMEM((4, T, QUART), BF16),
            pltpu.VMEM((ROWS, QUART), BF16),
            pltpu.VMEM((4, T, ROWS), BF16),
            pltpu.VMEM((T, ROWS), F32),
            pltpu.VMEM((4, T, ROWS), BF16),
            pltpu.VMEM((4, T, ROWS), BF16),
            pltpu.VMEM((ROWS, 4 * T), BF16),
            pltpu.VMEM((4, T, QUART), BF16),
            pltpu.VMEM((5, ROWS, COLS), BF16),
            pltpu.VMEM((3, ROWS, COLS), BF16),
            pltpu.VMEM((ROWS, COLS), BF16),
            pltpu.VMEM((FF, T), BF16),
            pltpu.VMEM((T, FF), BF16),
            pltpu.VMEM((FF, COLS), BF16),
            pltpu.VMEM((FF, COLS), F32),
            pltpu.VMEM((FF, COLS), F32),
            pltpu.VMEM((FF, COLS), BF16),
            pltpu.VMEM((8, YROWS, YCOLS), BF16),
            pltpu.VMEM((YROWS, YCOLS), F32),
            pltpu.VMEM((YROWS, YCOLS), F32),
            pltpu.VMEM((FF, COLS), F32),
            dma((8,)),
            dma((5,)),
            dma((11,)),
            dma((4,)), dma((4,)),
            dma((NG, 5)), dma((NG, 4)),
            dma((NG, 4)), dma((NG, 4)),
            dma((NG, 4)), dma((NG, 4)),
            dma((4, 2)), dma((4, 2)),
            dma((NG, 3)), dma((NG, 5)),
            dma((8,)), dma((8,)),
            dma((1,)), dma((1,)),
            dma((8,)), dma((8,)),
        ],
        compiler_params=pltpu.CompilerParams(
            collective_id=0, has_side_effects=True, vmem_limit_bytes=60 * 1024 * 1024
        ),
        cost_estimate=pl.CostEstimate(
            flops=11_300_000_000, bytes_accessed=16_000_000, transcendentals=T * FF
        ),
    )(tokens, hidden_grad.T, gate_next, up_next, inner_gate, anchor, momentum)
    return pl.pallas_call(
        results,
        out_shape=shapes,
        in_specs=[pl.BlockSpec(memory_space=pl.ANY)] * 5,
        out_specs=[pl.BlockSpec(memory_space=pl.ANY)] * 5,
        scratch_shapes=[
            pltpu.VMEM((T, D), BF16),
            pltpu.VMEM((1, FF, COLS), BF16),
            pltpu.VMEM((1, FF, COLS), BF16),
            pltpu.VMEM((FF, COLS), F32),
            pltpu.VMEM((FF, COLS), F32),
            dma((4 + PARTS,)),
            dma((4 + PARTS,)),
        ],
        compiler_params=pltpu.CompilerParams(vmem_limit_bytes=60 * 1024 * 1024),
    )(*outs)


def solution(mesh):
    return jax.shard_map(
        shards,
        mesh=mesh,
        in_specs=(
            P(("replica", "fsdp"), None),
            P(("replica", "fsdp"), None),
            P("replica", None, "fsdp"),
            P("replica", None, "fsdp"),
            P("replica", None, "fsdp"),
            P(None, "fsdp"),
            P(None, "fsdp"),
        ),
        out_specs=(
            P(("replica", "fsdp"), None),
            P("replica", None, "fsdp"),
            P("replica", None, "fsdp"),
            P(None, "fsdp"),
            P(None, "fsdp"),
        ),
        check_vma=False,
    )
```

```python
import functools
import jax
import jax.numpy as jnp
from jax import lax
from jax.experimental import pallas as pl
from jax.experimental.pallas import tpu as pltpu
from jax.sharding import PartitionSpec as P

MESH = pl.DeviceIdType.MESH
BF16 = jnp.bfloat16
F32 = jnp.float32

EPS = 1e-06
MU = 0.9
RATE = 0.7

T = 256
FF = 448
COLS = 512
QUART = 2048
D = 8192
RUN = 128

BLOCKS = ((0, 128), (128, 128), (256, 128), (384, 64))
GROUPS = ((0, 256), (256, 512), (512, 768), (768, 896))
ROWS = 896
NG = len(GROUPS)
RING = (False, True, True, True)
YROWS = 224
YCOLS = 128
PARTS = 8


def dot_nt(a, b):
    return lax.dot_general(a, b, (((1,), (1,)), ((), ())), preferred_element_type=F32)


def dot_nn(a, b):
    return lax.dot_general(a, b, (((1,), (0,)), ((), ())), preferred_element_type=F32)


def cots(gate, upval, cotan):
    sig = jax.nn.sigmoid(gate)
    gate_cot = cotan * upval * sig * (1.0 + gate * (1.0 - sig))
    up_cot = cotan * gate * sig
    return gate_cot, up_cot


def kernel(
    tokens, hgrad, gate_n, up_n, inner, anchor, momentum,
    tg_out, gg_out, ug_out, na_out, nm_out,
    xq, w, pst, pown, phop, prx, c, ct, tgs, rsi, rso, hgt, hg,
    inn, anc, mom, dec, yrx, ysum, zrx, tot,
    w_l, in_l, tok_s, tok_r, w_s, w_r, p_s, p_r, c_s, c_r, t_s, t_r, g_s, g_r,
    y_s, y_r, zh_s, zh_r, b_s, b_r,
):
    r = lax.axis_index("replica")
    f = lax.axis_index("fsdp")
    x, z = f // 4, f % 4
    zh, y, core = r // 8, (r // 2) % 4, r % 2
    low = z < 2
    end = (z == 0) | (z == 3)
    mid = (z == 1) | (z == 2)
    step = jnp.where(low, 1, -1)
    inward = (r, f + step)
    outward = (r, f - step)

    def xdev(k):
        return (r, ((x + k) % 4) * 4 + z)

    def ydev(dy, dc):
        return (zh * 8 + ((y + dy) % 4) * 2 + (core + dc) % 2, f)

    zpart = ((r + 8) % 16, f)
    ypeers = [(dy, dc) for dy in range(4) for dc in range(2) if (dy, dc) != (0, 0)]

    def colsz(zz):
        return pl.ds(pl.multiple_of(zz * COLS, COLS), COLS)

    def quart(xx):
        return pl.ds(pl.multiple_of(xx * QUART, QUART), QUART)

    w_local = []
    for b, (u0, n) in enumerate(BLOCKS):
        at = 2 * u0
        w_local.append(pltpu.make_async_copy(
            gate_n.at[0, pl.ds(u0, n)], w.at[pl.ds(at, n), colsz(z)], w_l.at[2 * b]))
        w_local.append(pltpu.make_async_copy(
            up_n.at[0, pl.ds(u0, n)], w.at[pl.ds(at + n, n), colsz(z)], w_l.at[2 * b + 1]))
    for q in w_local:
        q.start()
    own_tok = pltpu.make_async_copy(tokens.at[:, quart(x)], xq.at[0], in_l.at[0])
    in_inner = pltpu.make_async_copy(inner.at[0], inn, in_l.at[1])
    in_anchor = pltpu.make_async_copy(anchor, anc, in_l.at[2])
    in_mom = pltpu.make_async_copy(momentum, mom, in_l.at[3])
    in_hg = pltpu.make_async_copy(hgrad, hgt, in_l.at[4])
    for q in (own_tok, in_inner, in_anchor, in_mom, in_hg):
        q.start()

    barrier = pltpu.get_barrier_semaphore()

    def greet(dev):
        pl.semaphore_signal(barrier, inc=1, device_id=dev, device_id_type=MESH)

    for k in (1, 2, 3):
        greet(xdev(k))
    greet(inward)

    @pl.when(mid)
    def _():
        greet(outward)

    for dy, dc in ypeers:
        greet(ydev(dy, dc))
    greet(zpart)
    pl.semaphore_wait(barrier, 12 + jnp.where(mid, 1, 0))

    def remote(src, dst, ss, rs, dev):
        return pltpu.make_async_remote_copy(
            src_ref=src, dst_ref=dst, send_sem=ss, recv_sem=rs, device_id=dev, device_id_type=MESH)

    tok = {k: remote(tokens.at[:, quart((x + k) % 4)], xq.at[k], tok_s.at[k], tok_r.at[k], xdev(k))
           for k in (1, 2, 3)}
    for k in (2, 1, 3):
        tok[k].start()

    near_end = jnp.where(low, 0, 3)
    far_mid = jnp.where(low, 2, 1)
    far_end = jnp.where(low, 3, 0)

    def wpiece(g, origin, slot, dev):
        a, b = GROUPS[g]
        ref = w.at[pl.ds(a, b - a), colsz(origin)]
        return remote(ref, ref, w_s.at[g, slot], w_r.at[g, origin], dev)

    def w_wait_local(g):
        w_local[2 * g].wait()
        w_local[2 * g + 1].wait()

    def w_start():
        for g in range(NG):
            w_wait_local(g)

            @pl.when(end if g else end | mid)
            def _():
                wpiece(g, z, 0, inward).start()

            if g == 0:
                @pl.when(mid)
                def _():
                    wpiece(g, z, 1, outward).start()

    def w_near(g):
        @pl.when(mid)
        def _():
            wpiece(g, near_end, 2, inward).wait_recv()
            wpiece(g, near_end, 2, inward).start()
            wpiece(g, far_mid, 3, outward).wait_recv()
            wpiece(g, far_mid, 3, outward).start()
            if g + 1 < NG:
                wpiece(g + 1, z, 0, inward).start()
                wpiece(g + 1, z, 1, outward).start()

    def w_far(g):
        @pl.when(mid)
        def _():
            wpiece(g, far_end, 4, outward).wait_recv()
            wpiece(g, far_end, 4, outward).start()

    def w_here(g):
        @pl.when(end)
        def _():
            wpiece(g, z + step, 0, inward).wait_recv()
            wpiece(g, far_mid, 0, inward).wait_recv()
            wpiece(g, far_end, 0, inward).wait_recv()

    def w_drain(g):
        wpiece(g, z, 0, inward).wait_send()

        @pl.when(mid)
        def _():
            wpiece(g, z, 1, outward).wait_send()
            wpiece(g, near_end, 2, inward).wait_send()
            wpiece(g, far_mid, 3, outward).wait_send()
            wpiece(g, far_end, 4, outward).wait_send()

    def yslice(ref, yy, cc):
        return ref.at[pl.ds(pl.multiple_of(cc * YROWS, YROWS), YROWS),
                      pl.ds(pl.multiple_of(yy * YCOLS, YCOLS), YCOLS)]

    def yscatter(i):
        dy, dc = ypeers[i]
        slot = dy * 2 + dc
        return remote(yslice(dec, (y + dy) % 4, (core + dc) % 2), yrx.at[slot],
                      y_s.at[slot], y_r.at[slot], ydev(dy, dc))

    def ygather(i):
        dy, dc = ypeers[i]
        slot = dy * 2 + dc
        return remote(yslice(tot, y, core), yslice(tot, y, core), b_s.at[slot], b_r.at[slot], ydev(dy, dc))

    def ygather_in(i):
        dy, dc = ypeers[i]
        slot = dy * 2 + dc
        ref = yslice(tot, (y + 4 - dy) % 4, (core + dc) % 2)
        return remote(ref, ref, b_s.at[slot], b_r.at[slot], ydev(dy, dc))

    zswap = remote(ysum.at[...], zrx.at[...], zh_s.at[0], zh_r.at[0], zpart)

    def outer_decode():
        in_anchor.wait()
        in_inner.wait()
        for j in range(COLS // RUN):
            s = slice(j * RUN, (j + 1) * RUN)
            delta = anc[:, s] - inn[:, s].astype(F32)
            scale = jnp.max(jnp.abs(delta), axis=-1, keepdims=True) + EPS
            code = jnp.floor((delta / scale) * 7.0 + 0.5)
            dec[:, s] = (scale * code / 7.0).astype(BF16)
        for i in range(7):
            yscatter(i).start()

    def outer_sum():
        total = yslice(dec, y, core)[...].astype(F32)
        for i in range(7):
            yscatter(i).wait_recv()
        for i in range(7):
            dy, dc = ypeers[i]
            total = total + yrx[dy * 2 + dc].astype(F32)
        ysum[...] = total
        zswap.start()

    def outer_share():
        zswap.wait_recv()
        yslice(tot, y, core)[...] = ysum[...] + zrx[...]
        for i in range(7):
            ygather(i).start()

    def outer_finish():
        in_mom.wait()
        for i in range(7):
            ygather_in(i).wait_recv()
        grad = tot[...] / 16.0
        new_m = MU * mom[...] + grad
        nm_out[...] = new_m
        na_out[...] = anc[...] - RATE * (grad + MU * new_m)

    def lanes(g):
        a, b = GROUPS[g]
        return pl.ds(a, b - a)

    lower, upper = pl.ds(0, T // 2), pl.ds(T // 2, T // 2)

    def hop_copy(g, i):
        rows = (lower, upper)[i]
        return remote(pst.at[2, rows, lanes(g)], phop.at[rows, lanes(g)],
                      p_s.at[g, 2 * i], p_r.at[g, 2 * i], xdev((1, 3)[i]))

    def part_copy(g, k):
        return remote(pst.at[k, :, lanes(g)], prx.at[k // 2, :, lanes(g)], p_s.at[g, k], p_r.at[g, k], xdev(4 - k))

    def cot_copy(g, k):
        return remote(c.at[0, :, lanes(g)], c.at[k, :, lanes(g)], c_s.at[g, k], c_r.at[g, k], xdev(k))

    def cot_hop(g, i):
        rows = (lower, upper)[i]
        return remote(c.at[(1, 3)[i], rows, lanes(g)], c.at[2, rows, lanes(g)],
                      c_s.at[g, 2 * i], c_r.at[g, 2 * i], xdev((1, 3)[i]))

    def part_far(g):
        return remote(pst.at[2, :, lanes(g)], phop.at[:, lanes(g)], p_s.at[g, 0], p_r.at[g, 0], xdev(2))

    def opposite(g):
        a, b = GROUPS[g]
        pst[2, :, a:b] = dot_nt(xq[2], w[a:b, :]).astype(BF16)
        if not RING[g]:
            part_far(g).start()
            return
        for i in range(2):
            hop_copy(g, i).start()

    def neighbours(g):
        a, b = GROUPS[g]
        half = T // 2
        for i, k in enumerate((3, 1)):
            rows = slice(i * half, (i + 1) * half)
            other = slice((1 - i) * half, (2 - i) * half)
            part = dot_nt(xq[k], w[a:b, :])
            if RING[g]:
                hop_copy(g, i).wait_recv()
                pst[k, rows, a:b] = (part[rows] + phop[rows, a:b].astype(F32)).astype(BF16)
                pst[k, other, a:b] = part[other].astype(BF16)
            else:
                pst[k, :, a:b] = part.astype(BF16)
            part_copy(g, k).start()

    def own_part(g):
        a, b = GROUPS[g]
        pown[:, a:b] = dot_nt(xq[0], w[a:b, :])

    def owner(g):
        a, b = GROUPS[g]
        for k in (3, 1):
            part_copy(g, k).wait_recv()
        if not RING[g]:
            part_far(g).wait_recv()
        for u0, n in BLOCKS:
            at = 2 * u0
            if not a <= at < b:
                continue
            full = slice(at, at + 2 * n)
            total = pown[:, full] + prx[0, :, full].astype(F32) + prx[1, :, full].astype(F32)
            if not RING[g]:
                total = total + phop[:, full].astype(F32)
            if n == 128:
                gc, uc = cots(total[:, :n], total[:, n:], hg[:, u0:u0 + n].astype(F32))
                c[0, :, at:at + n] = gc.astype(BF16)
                c[0, :, at + n:at + 2 * n] = uc.astype(BF16)
            else:
                part = hg[:, u0:u0 + n].astype(F32)
                cotan = jnp.concatenate([part, part], axis=1)
                turned = pltpu.roll(total, n, 1)
                first = lax.broadcasted_iota(jnp.int32, total.shape, 1) < n
                gc, uc = cots(jnp.where(first, total, turned), jnp.where(first, turned, total), cotan)
                c[0, :, full] = jnp.where(first, gc, uc).astype(BF16)
        for k in (1, 3) if RING[g] else (2, 1, 3):
            cot_copy(g, k).start()

    def cot_pass(g):
        for i, k in enumerate((1, 3)):
            cot_copy(g, k).wait_recv()
            cot_hop(g, i).start()

    def cot_last(g):
        if not RING[g]:
            cot_copy(g, 2).wait_recv()
            return
        for i in range(2):
            cot_hop(g, i).wait_recv()

    def turn(g):
        a, b = GROUPS[g]
        for k in range(4):
            ct[a:b, k * T:(k + 1) * T] = c[k, :, a:b].T

    def gathered(g):
        a, b = GROUPS[g]
        if not RING[g]:
            for k in (1, 3):
                cot_copy(g, k).wait_recv()
        for k in (0, 1, 3):
            ct[a:b, k * T:(k + 1) * T] = c[k, :, a:b].T
        cot_last(g)
        ct[a:b, 2 * T:3 * T] = c[2, :, a:b].T

    dest_a = jnp.where(low, 3, 0)
    dest_b = jnp.where(low, 2, 1)
    dest_c = jnp.where(z == 0, 1, jnp.where(z == 1, 0, jnp.where(z == 2, 3, 2)))
    dev_c = (r, f + jnp.where(end, step, -step))
    slot_a = jnp.where(end, 0, 3)
    slot_b = jnp.where(end, 1, 4)
    sends = ((dest_a, inward, slot_a, 0), (dest_b, inward, slot_b, 1), (dest_c, dev_c, 2, 3))

    def grad_copy(g, i):
        a, b = GROUPS[g]
        dest, dev, slot, _ = sends[i]
        return remote(rso.at[i, pl.ds(a, b - a)], rsi.at[slot, pl.ds(a, b - a)],
                      g_s.at[g, i], g_r.at[g, slot], dev)

    def grad_in(g, slot):
        a, b = GROUPS[g]
        ref = rsi.at[slot, pl.ds(a, b - a)]
        return remote(ref, ref, g_s.at[g, 0], g_r.at[g, slot], inward)

    def grad_term(g, dest):
        a, b = GROUPS[g]
        return dot_nn(ct[a:b, :], xq[:, :, colsz(dest)].reshape(4 * T, COLS))

    def grad_send(g, i):
        a, b = GROUPS[g]
        dest, _, _, arrives = sends[i]
        rso[i, a:b] = grad_term(g, dest).astype(BF16)

        @pl.when(mid)
        def _():
            grad_in(g, arrives).wait_recv()
            rso[i, a:b] = (rso[i, a:b].astype(F32) + rsi[arrives, a:b].astype(F32)).astype(BF16)

        grad_copy(g, i).start()

    def grad_own(g):
        a, b = GROUPS[g]
        pown2 = grad_term(g, z)
        grad_in(g, 2).wait_recv()
        pown2 = pown2 + rsi[2, a:b].astype(F32)

        @pl.when(mid)
        def _():
            grad_in(g, 4).wait_recv()
            put(g, pown2 + rsi[4, a:b].astype(F32))

        @pl.when(end)
        def _():
            put(g, pown2)

    def put(g, total):
        a, b = GROUPS[g]
        for u0, n in BLOCKS:
            at = 2 * u0 - a
            if 0 <= at < b - a:
                gg_out[0, u0:u0 + n] = total[at:at + n].astype(BF16)
                ug_out[0, u0:u0 + n] = total[at + n:at + 2 * n].astype(BF16)

    def tg_cols(xx, h):
        return pl.ds(pl.multiple_of(xx * QUART + h * (QUART // 2), QUART // 2), QUART // 2)

    def tg_copy(k, h):
        return remote(tgs.at[k, :, pl.ds(h * (QUART // 2), QUART // 2)], tg_out.at[:, tg_cols(x, h)],
                      t_s.at[k, h], t_r.at[k, h], xdev(4 - k))

    def tg_in(k, h):
        return remote(tgs.at[k, :, pl.ds(h * (QUART // 2), QUART // 2)], tg_out.at[:, tg_cols((x + k) % 4, h)],
                      t_s.at[k, h], t_r.at[k, h], xdev(4 - k))

    def token_grad(k, h):
        for j in (2 * h, 2 * h + 1):
            s = slice(j * COLS, (j + 1) * COLS)
            part = dot_nn(c[k], w[:, s]).astype(BF16)
            if k:
                tgs[k, :, s] = part
            else:
                tg_out[:, pl.ds(pl.multiple_of(x * QUART + j * COLS, COLS), COLS)] = part
        if k:
            tg_copy(k, h).start()

    w_start()
    outer_decode()
    w_near(0)
    in_hg.wait()
    hg[...] = hgt[...].T
    w_far(0)
    w_near(1)
    outer_sum()
    own_tok.wait()
    w_here(0)
    tok[2].wait_recv()
    opposite(0)
    w_far(1)
    own_part(0)
    w_near(2)
    outer_share()
    w_far(2)
    w_near(3)
    w_here(1)
    own_part(1)
    outer_finish()
    w_far(3)
    tok[1].wait_recv()
    tok[3].wait_recv()
    neighbours(0)
    opposite(1)
    owner(0)
    neighbours(1)
    w_here(2)
    opposite(2)
    own_part(2)
    gathered(0)
    for i in range(3):
        @pl.when(end)
        def _():
            grad_send(0, i)
    w_here(3)
    opposite(3)
    own_part(3)
    owner(1)
    neighbours(2)
    neighbours(3)
    cot_pass(1)
    owner(2)
    owner(3)
    gathered(1)
    for i in range(3):
        @pl.when(end)
        def _():
            grad_send(1, i)
    for i in range(2):
        @pl.when(mid)
        def _():
            grad_send(0, i)
    cot_pass(2)
    cot_pass(3)
    cot_last(2)
    token_grad(1, 0)
    token_grad(3, 0)
    cot_last(3)
    for k, h in ((2, 0), (2, 1), (1, 1), (3, 1)):
        token_grad(k, h)
    turn(2)
    turn(3)

    @pl.when(mid)
    def _():
        grad_send(0, 2)
    for i in range(3):
        @pl.when(mid)
        def _():
            grad_send(1, i)
    for i in range(3):
        grad_send(2, i)
    for i in range(3):
        grad_send(3, i)
    token_grad(0, 0)
    token_grad(0, 1)
    for g in range(4):
        grad_own(g)

    for k in (1, 3, 2):
        for h in range(2):
            tg_in(k, h).wait_recv()
    for k in (1, 2, 3):
        tok[k].wait_send()
        for h in range(2):
            tg_copy(k, h).wait_send()
        for g in range(NG):
            if k != 2:
                part_copy(g, k).wait_send()
                cot_copy(g, k).wait_send()
    for g in range(NG):
        w_drain(g)
        if RING[g]:
            for i in range(2):
                hop_copy(g, i).wait_send()
                cot_hop(g, i).wait_send()
        else:
            part_far(g).wait_send()
            cot_copy(g, 2).wait_send()
        for i in range(3):
            grad_copy(g, i).wait_send()
    for i in range(7):
        yscatter(i).wait_send()
        ygather(i).wait_send()
    zswap.wait_send()


def results(tg, gg, ug, na, nm, tg_out, gg_out, ug_out, na_out, nm_out, out_s):
    ways = [(na, na_out), (nm, nm_out), (gg, gg_out), (ug, ug_out)]
    for i in range(PARTS):
        rows = pl.ds(i * (T // PARTS), T // PARTS)
        ways.append((tg.at[rows], tg_out.at[rows]))
    outs = [pltpu.make_async_copy(src, dst, out_s.at[i]) for i, (src, dst) in enumerate(ways)]
    for o in outs:
        o.start()
    for o in outs:
        o.wait()


def shards(tokens, hidden_grad, gate_next, up_next, inner_gate, anchor, momentum):
    dma = pltpu.SemaphoreType.DMA
    shapes = (
        jax.ShapeDtypeStruct((T, D), BF16),
        jax.ShapeDtypeStruct((1, FF, COLS), BF16),
        jax.ShapeDtypeStruct((1, FF, COLS), BF16),
        jax.ShapeDtypeStruct((FF, COLS), F32),
        jax.ShapeDtypeStruct((FF, COLS), F32),
    )
    outs = pl.pallas_call(
        kernel,
        out_shape=tuple(pltpu.VMEM(o.shape, o.dtype) for o in shapes),
        in_specs=[pl.BlockSpec(memory_space=pltpu.HBM)] * 7,
        out_specs=[pl.BlockSpec(memory_space=pltpu.VMEM)] * 5,
        scratch_shapes=[
            pltpu.VMEM((4, T, QUART), BF16),
            pltpu.VMEM((ROWS, QUART), BF16),
            pltpu.VMEM((4, T, ROWS), BF16),
            pltpu.VMEM((T, ROWS), F32),
            pltpu.VMEM((T, ROWS), BF16),
            pltpu.VMEM((2, T, ROWS), BF16),
            pltpu.VMEM((4, T, ROWS), BF16),
            pltpu.VMEM((ROWS, 4 * T), BF16),
            pltpu.VMEM((4, T, QUART), BF16),
            pltpu.VMEM((5, ROWS, COLS), BF16),
            pltpu.VMEM((3, ROWS, COLS), BF16),
            pltpu.VMEM((FF, T), BF16),
            pltpu.VMEM((T, FF), BF16),
            pltpu.VMEM((FF, COLS), BF16),
            pltpu.VMEM((FF, COLS), F32),
            pltpu.VMEM((FF, COLS), F32),
            pltpu.VMEM((FF, COLS), BF16),
            pltpu.VMEM((8, YROWS, YCOLS), BF16),
            pltpu.VMEM((YROWS, YCOLS), F32),
            pltpu.VMEM((YROWS, YCOLS), F32),
            pltpu.VMEM((FF, COLS), F32),
            dma((8,)),
            dma((5,)),
            dma((4,)), dma((4,)),
            dma((NG, 5)), dma((NG, 4)),
            dma((NG, 4)), dma((NG, 4)),
            dma((NG, 4)), dma((NG, 4)),
            dma((4, 2)), dma((4, 2)),
            dma((NG, 3)), dma((NG, 5)),
            dma((8,)), dma((8,)),
            dma((1,)), dma((1,)),
            dma((8,)), dma((8,)),
        ],
        compiler_params=pltpu.CompilerParams(
            collective_id=0, has_side_effects=True, vmem_limit_bytes=54 * 1024 * 1024
        ),
        cost_estimate=pl.CostEstimate(
            flops=11_300_000_000, bytes_accessed=16_000_000, transcendentals=T * FF
        ),
    )(tokens, hidden_grad.T, gate_next, up_next, inner_gate, anchor, momentum)
    return pl.pallas_call(
        results,
        out_shape=shapes,
        in_specs=[pl.BlockSpec(memory_space=pltpu.VMEM)] * 5,
        out_specs=[pl.BlockSpec(memory_space=pl.ANY)] * 5,
        scratch_shapes=[dma((4 + PARTS,))],
        compiler_params=pltpu.CompilerParams(vmem_limit_bytes=16 * 1024 * 1024),
    )(*outs)


def solution(mesh):
    return jax.shard_map(
        shards,
        mesh=mesh,
        in_specs=(
            P(("replica", "fsdp"), None),
            P(("replica", "fsdp"), None),
            P("replica", None, "fsdp"),
            P("replica", None, "fsdp"),
            P("replica", None, "fsdp"),
            P(None, "fsdp"),
            P(None, "fsdp"),
        ),
        out_specs=(
            P(("replica", "fsdp"), None),
            P("replica", None, "fsdp"),
            P("replica", None, "fsdp"),
            P(None, "fsdp"),
            P(None, "fsdp"),
        ),
        check_vma=False,
    )
```

```python
import functools
import jax
import jax.numpy as jnp
from jax import lax
from jax.experimental import pallas as pl
from jax.experimental.pallas import tpu as pltpu
from jax.sharding import PartitionSpec as P

MESH = pl.DeviceIdType.MESH
BF16 = jnp.bfloat16
F32 = jnp.float32

EPS = 1e-06
MU = 0.9
RATE = 0.7

T = 256
FF = 448
COLS = 512
QUART = 2048
D = 8192
RUN = 128

BLOCKS = ((0, 128), (128, 128), (256, 128), (384, 64))
GROUPS = ((0, 256), (256, 512), (512, 768), (768, 896))
ROWS = 896
NG = len(GROUPS)
RING = (False, True, True, True)
YROWS = 224
YCOLS = 128
PARTS = 8


def dot_nt(a, b):
    return lax.dot_general(a, b, (((1,), (1,)), ((), ())), preferred_element_type=F32)


def dot_nn(a, b):
    return lax.dot_general(a, b, (((1,), (0,)), ((), ())), preferred_element_type=F32)


def cots(gate, upval, cotan):
    sig = jax.nn.sigmoid(gate)
    gate_cot = cotan * upval * sig * (1.0 + gate * (1.0 - sig))
    up_cot = cotan * gate * sig
    return gate_cot, up_cot


def kernel(
    tokens, hgrad, gate_n, up_n, inner, anchor, momentum,
    tg_out, gg_out, ug_out, na_out, nm_out,
    xq, w, pst, pown, phop, prx, c, ct, tgs, rsi, rso, hgt, hg,
    inn, anc, mom, dec, yrx, ysum, zrx, tot,
    w_l, in_l, tok_s, tok_r, w_s, w_r, p_s, p_r, c_s, c_r, t_s, t_r, g_s, g_r,
    y_s, y_r, zh_s, zh_r, b_s, b_r,
):
    r = lax.axis_index("replica")
    f = lax.axis_index("fsdp")
    x, z = f // 4, f % 4
    zh, y, core = r // 8, (r // 2) % 4, r % 2
    low = z < 2
    end = (z == 0) | (z == 3)
    mid = (z == 1) | (z == 2)
    step = jnp.where(low, 1, -1)
    inward = (r, f + step)
    outward = (r, f - step)

    def xdev(k):
        return (r, ((x + k) % 4) * 4 + z)

    def ydev(dy, dc):
        return (zh * 8 + ((y + dy) % 4) * 2 + (core + dc) % 2, f)

    zpart = ((r + 8) % 16, f)
    ypeers = [(dy, dc) for dy in range(4) for dc in range(2) if (dy, dc) != (0, 0)]

    def colsz(zz):
        return pl.ds(pl.multiple_of(zz * COLS, COLS), COLS)

    def quart(xx):
        return pl.ds(pl.multiple_of(xx * QUART, QUART), QUART)

    barrier = pltpu.get_barrier_semaphore()

    def greet(dev):
        pl.semaphore_signal(barrier, inc=1, device_id=dev, device_id_type=MESH)

    for k in (1, 2, 3):
        greet(xdev(k))
    greet(inward)

    @pl.when(mid)
    def _():
        greet(outward)

    for dy, dc in ypeers:
        greet(ydev(dy, dc))
    greet(zpart)
    w_local = []
    for b, (u0, n) in enumerate(BLOCKS):
        at = 2 * u0
        w_local.append(pltpu.make_async_copy(
            gate_n.at[0, pl.ds(u0, n)], w.at[pl.ds(at, n), colsz(z)], w_l.at[2 * b]))
        w_local.append(pltpu.make_async_copy(
            up_n.at[0, pl.ds(u0, n)], w.at[pl.ds(at + n, n), colsz(z)], w_l.at[2 * b + 1]))
    for q in w_local:
        q.start()
    own_tok = pltpu.make_async_copy(tokens.at[:, quart(x)], xq.at[0], in_l.at[0])
    in_inner = pltpu.make_async_copy(inner.at[0], inn, in_l.at[1])
    in_anchor = pltpu.make_async_copy(anchor, anc, in_l.at[2])
    in_mom = pltpu.make_async_copy(momentum, mom, in_l.at[3])
    in_hg = pltpu.make_async_copy(hgrad, hgt, in_l.at[4])
    for q in (own_tok, in_inner, in_anchor, in_mom, in_hg):
        q.start()

    pl.semaphore_wait(barrier, 12 + jnp.where(mid, 1, 0))

    def remote(src, dst, ss, rs, dev):
        return pltpu.make_async_remote_copy(
            src_ref=src, dst_ref=dst, send_sem=ss, recv_sem=rs, device_id=dev, device_id_type=MESH)

    tok = {k: remote(tokens.at[:, quart((x + k) % 4)], xq.at[k], tok_s.at[k], tok_r.at[k], xdev(k))
           for k in (1, 2, 3)}
    for k in (2, 1, 3):
        tok[k].start()

    near_end = jnp.where(low, 0, 3)
    far_mid = jnp.where(low, 2, 1)
    far_end = jnp.where(low, 3, 0)

    def wpiece(g, origin, slot, dev):
        a, b = GROUPS[g]
        ref = w.at[pl.ds(a, b - a), colsz(origin)]
        return remote(ref, ref, w_s.at[g, slot], w_r.at[g, origin], dev)

    def w_wait_local(g):
        w_local[2 * g].wait()
        w_local[2 * g + 1].wait()

    def w_start():
        for g in range(NG):
            w_wait_local(g)

            @pl.when(end if g else end | mid)
            def _():
                wpiece(g, z, 0, inward).start()

            if g == 0:
                @pl.when(mid)
                def _():
                    wpiece(g, z, 1, outward).start()

    def w_near(g):
        @pl.when(mid)
        def _():
            wpiece(g, near_end, 2, inward).wait_recv()
            wpiece(g, near_end, 2, inward).start()
            wpiece(g, far_mid, 3, outward).wait_recv()
            wpiece(g, far_mid, 3, outward).start()
            if g + 1 < NG:
                wpiece(g + 1, z, 0, inward).start()
                wpiece(g + 1, z, 1, outward).start()

    def w_far(g):
        @pl.when(mid)
        def _():
            wpiece(g, far_end, 4, outward).wait_recv()
            wpiece(g, far_end, 4, outward).start()

    def w_here(g):
        @pl.when(end)
        def _():
            wpiece(g, z + step, 0, inward).wait_recv()
            wpiece(g, far_mid, 0, inward).wait_recv()
            wpiece(g, far_end, 0, inward).wait_recv()

    def w_drain(g):
        wpiece(g, z, 0, inward).wait_send()

        @pl.when(mid)
        def _():
            wpiece(g, z, 1, outward).wait_send()
            wpiece(g, near_end, 2, inward).wait_send()
            wpiece(g, far_mid, 3, outward).wait_send()
            wpiece(g, far_end, 4, outward).wait_send()

    def yslice(ref, yy, cc):
        return ref.at[pl.ds(pl.multiple_of(cc * YROWS, YROWS), YROWS),
                      pl.ds(pl.multiple_of(yy * YCOLS, YCOLS), YCOLS)]

    def yscatter(i):
        dy, dc = ypeers[i]
        slot = dy * 2 + dc
        return remote(yslice(dec, (y + dy) % 4, (core + dc) % 2), yrx.at[slot],
                      y_s.at[slot], y_r.at[slot], ydev(dy, dc))

    def ygather(i):
        dy, dc = ypeers[i]
        slot = dy * 2 + dc
        return remote(yslice(tot, y, core), yslice(tot, y, core), b_s.at[slot], b_r.at[slot], ydev(dy, dc))

    def ygather_in(i):
        dy, dc = ypeers[i]
        slot = dy * 2 + dc
        ref = yslice(tot, (y + 4 - dy) % 4, (core + dc) % 2)
        return remote(ref, ref, b_s.at[slot], b_r.at[slot], ydev(dy, dc))

    zswap = remote(ysum.at[...], zrx.at[...], zh_s.at[0], zh_r.at[0], zpart)

    def outer_decode():
        in_anchor.wait()
        in_inner.wait()
        for j in range(COLS // RUN):
            s = slice(j * RUN, (j + 1) * RUN)
            delta = anc[:, s] - inn[:, s].astype(F32)
            scale = jnp.max(jnp.abs(delta), axis=-1, keepdims=True) + EPS
            code = jnp.floor((delta / scale) * 7.0 + 0.5)
            dec[:, s] = (scale * code / 7.0).astype(BF16)
        for i in range(7):
            yscatter(i).start()

    def outer_sum():
        total = yslice(dec, y, core)[...].astype(F32)
        for i in range(7):
            yscatter(i).wait_recv()
        for i in range(7):
            dy, dc = ypeers[i]
            total = total + yrx[dy * 2 + dc].astype(F32)
        ysum[...] = total
        zswap.start()

    def outer_share():
        zswap.wait_recv()
        yslice(tot, y, core)[...] = ysum[...] + zrx[...]
        for i in range(7):
            ygather(i).start()

    def outer_finish():
        in_mom.wait()
        for i in range(7):
            ygather_in(i).wait_recv()
        grad = tot[...] / 16.0
        new_m = MU * mom[...] + grad
        nm_out[...] = new_m
        na_out[...] = anc[...] - RATE * (grad + MU * new_m)

    def lanes(g):
        a, b = GROUPS[g]
        return pl.ds(a, b - a)

    lower, upper = pl.ds(0, T // 2), pl.ds(T // 2, T // 2)

    def hop_copy(g, i):
        rows = (lower, upper)[i]
        return remote(pst.at[2, rows, lanes(g)], phop.at[rows, lanes(g)],
                      p_s.at[g, 2 * i], p_r.at[g, 2 * i], xdev((1, 3)[i]))

    def part_copy(g, k):
        return remote(pst.at[k, :, lanes(g)], prx.at[k // 2, :, lanes(g)], p_s.at[g, k], p_r.at[g, k], xdev(4 - k))

    def cot_copy(g, k):
        return remote(c.at[0, :, lanes(g)], c.at[k, :, lanes(g)], c_s.at[g, k], c_r.at[g, k], xdev(k))

    def cot_hop(g, i):
        rows = (lower, upper)[i]
        return remote(c.at[(1, 3)[i], rows, lanes(g)], c.at[2, rows, lanes(g)],
                      c_s.at[g, 2 * i], c_r.at[g, 2 * i], xdev((1, 3)[i]))

    def part_far(g):
        return remote(pst.at[2, :, lanes(g)], phop.at[:, lanes(g)], p_s.at[g, 0], p_r.at[g, 0], xdev(2))

    def opposite(g):
        a, b = GROUPS[g]
        pst[2, :, a:b] = dot_nt(xq[2], w[a:b, :]).astype(BF16)
        if not RING[g]:
            part_far(g).start()
            return
        for i in range(2):
            hop_copy(g, i).start()

    def neighbours(g):
        a, b = GROUPS[g]
        half = T // 2
        for i, k in enumerate((3, 1)):
            rows = slice(i * half, (i + 1) * half)
            other = slice((1 - i) * half, (2 - i) * half)
            part = dot_nt(xq[k], w[a:b, :])
            if RING[g]:
                hop_copy(g, i).wait_recv()
                pst[k, rows, a:b] = (part[rows] + phop[rows, a:b].astype(F32)).astype(BF16)
                pst[k, other, a:b] = part[other].astype(BF16)
            else:
                pst[k, :, a:b] = part.astype(BF16)
            part_copy(g, k).start()

    def own_part(g):
        a, b = GROUPS[g]
        pown[:, a:b] = dot_nt(xq[0], w[a:b, :])

    def owner(g):
        a, b = GROUPS[g]
        for k in (3, 1):
            part_copy(g, k).wait_recv()
        if not RING[g]:
            part_far(g).wait_recv()
        for u0, n in BLOCKS:
            at = 2 * u0
            if not a <= at < b:
                continue
            full = slice(at, at + 2 * n)
            total = pown[:, full] + prx[0, :, full].astype(F32) + prx[1, :, full].astype(F32)
            if not RING[g]:
                total = total + phop[:, full].astype(F32)
            if n == 128:
                gc, uc = cots(total[:, :n], total[:, n:], hg[:, u0:u0 + n].astype(F32))
                c[0, :, at:at + n] = gc.astype(BF16)
                c[0, :, at + n:at + 2 * n] = uc.astype(BF16)
            else:
                part = hg[:, u0:u0 + n].astype(F32)
                cotan = jnp.concatenate([part, part], axis=1)
                turned = pltpu.roll(total, n, 1)
                first = lax.broadcasted_iota(jnp.int32, total.shape, 1) < n
                gc, uc = cots(jnp.where(first, total, turned), jnp.where(first, turned, total), cotan)
                c[0, :, full] = jnp.where(first, gc, uc).astype(BF16)
        for k in (1, 3) if RING[g] else (2, 1, 3):
            cot_copy(g, k).start()

    def cot_pass(g):
        for i, k in enumerate((1, 3)):
            cot_copy(g, k).wait_recv()
            cot_hop(g, i).start()

    def cot_last(g):
        if not RING[g]:
            cot_copy(g, 2).wait_recv()
            return
        for i in range(2):
            cot_hop(g, i).wait_recv()

    def turn(g):
        a, b = GROUPS[g]
        for k in range(4):
            ct[a:b, k * T:(k + 1) * T] = c[k, :, a:b].T

    def gathered(g):
        a, b = GROUPS[g]
        if not RING[g]:
            for k in (1, 3):
                cot_copy(g, k).wait_recv()
        for k in (0, 1, 3):
            ct[a:b, k * T:(k + 1) * T] = c[k, :, a:b].T
        cot_last(g)
        ct[a:b, 2 * T:3 * T] = c[2, :, a:b].T

    dest_a = jnp.where(low, 3, 0)
    dest_b = jnp.where(low, 2, 1)
    dest_c = jnp.where(z == 0, 1, jnp.where(z == 1, 0, jnp.where(z == 2, 3, 2)))
    dev_c = (r, f + jnp.where(end, step, -step))
    slot_a = jnp.where(end, 0, 3)
    slot_b = jnp.where(end, 1, 4)
    sends = ((dest_a, inward, slot_a, 0), (dest_b, inward, slot_b, 1), (dest_c, dev_c, 2, 3))

    def grad_copy(g, i):
        a, b = GROUPS[g]
        dest, dev, slot, _ = sends[i]
        return remote(rso.at[i, pl.ds(a, b - a)], rsi.at[slot, pl.ds(a, b - a)],
                      g_s.at[g, i], g_r.at[g, slot], dev)

    def grad_in(g, slot):
        a, b = GROUPS[g]
        ref = rsi.at[slot, pl.ds(a, b - a)]
        return remote(ref, ref, g_s.at[g, 0], g_r.at[g, slot], inward)

    def grad_term(g, dest):
        a, b = GROUPS[g]
        return dot_nn(ct[a:b, :], xq[:, :, colsz(dest)].reshape(4 * T, COLS))

    def grad_send(g, i):
        a, b = GROUPS[g]
        dest, _, _, arrives = sends[i]
        rso[i, a:b] = grad_term(g, dest).astype(BF16)

        @pl.when(mid)
        def _():
            grad_in(g, arrives).wait_recv()
            rso[i, a:b] = (rso[i, a:b].astype(F32) + rsi[arrives, a:b].astype(F32)).astype(BF16)

        grad_copy(g, i).start()

    def grad_own(g):
        a, b = GROUPS[g]
        pown2 = grad_term(g, z)
        grad_in(g, 2).wait_recv()
        pown2 = pown2 + rsi[2, a:b].astype(F32)

        @pl.when(mid)
        def _():
            grad_in(g, 4).wait_recv()
            put(g, pown2 + rsi[4, a:b].astype(F32))

        @pl.when(end)
        def _():
            put(g, pown2)

    def put(g, total):
        a, b = GROUPS[g]
        for u0, n in BLOCKS:
            at = 2 * u0 - a
            if 0 <= at < b - a:
                gg_out[0, u0:u0 + n] = total[at:at + n].astype(BF16)
                ug_out[0, u0:u0 + n] = total[at + n:at + 2 * n].astype(BF16)

    def tg_cols(xx, h):
        return pl.ds(pl.multiple_of(xx * QUART + h * (QUART // 2), QUART // 2), QUART // 2)

    def tg_copy(k, h):
        return remote(tgs.at[k, :, pl.ds(h * (QUART // 2), QUART // 2)], tg_out.at[:, tg_cols(x, h)],
                      t_s.at[k, h], t_r.at[k, h], xdev(4 - k))

    def tg_in(k, h):
        return remote(tgs.at[k, :, pl.ds(h * (QUART // 2), QUART // 2)], tg_out.at[:, tg_cols((x + k) % 4, h)],
                      t_s.at[k, h], t_r.at[k, h], xdev(4 - k))

    def token_grad(k, h):
        for j in (2 * h, 2 * h + 1):
            s = slice(j * COLS, (j + 1) * COLS)
            part = dot_nn(c[k], w[:, s]).astype(BF16)
            if k:
                tgs[k, :, s] = part
            else:
                tg_out[:, pl.ds(pl.multiple_of(x * QUART + j * COLS, COLS), COLS)] = part
        if k:
            tg_copy(k, h).start()

    w_start()
    outer_decode()
    w_near(0)
    in_hg.wait()
    hg[...] = hgt[...].T
    w_far(0)
    outer_sum()
    w_near(1)
    own_tok.wait()
    w_here(0)
    tok[2].wait_recv()
    opposite(0)
    w_far(1)
    own_part(0)
    w_near(2)
    w_far(2)
    w_near(3)
    w_here(1)
    own_part(1)
    w_far(3)
    tok[1].wait_recv()
    tok[3].wait_recv()
    neighbours(0)
    opposite(1)
    owner(0)
    neighbours(1)
    w_here(2)
    opposite(2)
    own_part(2)
    gathered(0)
    for i in range(3):
        @pl.when(end)
        def _():
            grad_send(0, i)
    w_here(3)
    opposite(3)
    own_part(3)
    outer_share()
    owner(1)
    neighbours(2)
    neighbours(3)
    cot_pass(1)
    owner(2)
    owner(3)
    gathered(1)
    for i in range(3):
        @pl.when(end)
        def _():
            grad_send(1, i)
    for i in range(2):
        @pl.when(mid)
        def _():
            grad_send(0, i)
    cot_pass(2)
    cot_pass(3)
    cot_last(2)
    token_grad(1, 0)
    token_grad(3, 0)
    cot_last(3)
    for k, h in ((2, 0), (2, 1), (1, 1), (3, 1)):
        token_grad(k, h)
    turn(2)
    turn(3)

    @pl.when(mid)
    def _():
        grad_send(0, 2)
    for i in range(3):
        @pl.when(mid)
        def _():
            grad_send(1, i)
    for i in range(3):
        grad_send(2, i)
    for i in range(3):
        grad_send(3, i)
    token_grad(0, 0)
    token_grad(0, 1)
    outer_finish()
    for g in range(4):
        grad_own(g)

    for k in (1, 3, 2):
        for h in range(2):
            tg_in(k, h).wait_recv()
    for k in (1, 2, 3):
        tok[k].wait_send()
        for h in range(2):
            tg_copy(k, h).wait_send()
        for g in range(NG):
            if k != 2:
                part_copy(g, k).wait_send()
                cot_copy(g, k).wait_send()
    for g in range(NG):
        w_drain(g)
        if RING[g]:
            for i in range(2):
                hop_copy(g, i).wait_send()
                cot_hop(g, i).wait_send()
        else:
            part_far(g).wait_send()
            cot_copy(g, 2).wait_send()
        for i in range(3):
            grad_copy(g, i).wait_send()
    for i in range(7):
        yscatter(i).wait_send()
        ygather(i).wait_send()
    zswap.wait_send()


def results(tg, gg, ug, na, nm, tg_out, gg_out, ug_out, na_out, nm_out, out_s):
    ways = [(na, na_out), (nm, nm_out), (gg, gg_out), (ug, ug_out)]
    for i in range(PARTS):
        rows = pl.ds(i * (T // PARTS), T // PARTS)
        ways.append((tg.at[rows], tg_out.at[rows]))
    outs = [pltpu.make_async_copy(src, dst, out_s.at[i]) for i, (src, dst) in enumerate(ways)]
    for o in outs:
        o.start()
    for o in outs:
        o.wait()


def shards(tokens, hidden_grad, gate_next, up_next, inner_gate, anchor, momentum):
    dma = pltpu.SemaphoreType.DMA
    shapes = (
        jax.ShapeDtypeStruct((T, D), BF16),
        jax.ShapeDtypeStruct((1, FF, COLS), BF16),
        jax.ShapeDtypeStruct((1, FF, COLS), BF16),
        jax.ShapeDtypeStruct((FF, COLS), F32),
        jax.ShapeDtypeStruct((FF, COLS), F32),
    )
    outs = pl.pallas_call(
        kernel,
        out_shape=tuple(pltpu.VMEM(o.shape, o.dtype) for o in shapes),
        in_specs=[pl.BlockSpec(memory_space=pltpu.HBM)] * 7,
        out_specs=[pl.BlockSpec(memory_space=pltpu.VMEM)] * 5,
        scratch_shapes=[
            pltpu.VMEM((4, T, QUART), BF16),
            pltpu.VMEM((ROWS, QUART), BF16),
            pltpu.VMEM((4, T, ROWS), BF16),
            pltpu.VMEM((T, ROWS), F32),
            pltpu.VMEM((T, ROWS), BF16),
            pltpu.VMEM((2, T, ROWS), BF16),
            pltpu.VMEM((4, T, ROWS), BF16),
            pltpu.VMEM((ROWS, 4 * T), BF16),
            pltpu.VMEM((4, T, QUART), BF16),
            pltpu.VMEM((5, ROWS, COLS), BF16),
            pltpu.VMEM((3, ROWS, COLS), BF16),
            pltpu.VMEM((FF, T), BF16),
            pltpu.VMEM((T, FF), BF16),
            pltpu.VMEM((FF, COLS), BF16),
            pltpu.VMEM((FF, COLS), F32),
            pltpu.VMEM((FF, COLS), F32),
            pltpu.VMEM((FF, COLS), BF16),
            pltpu.VMEM((8, YROWS, YCOLS), BF16),
            pltpu.VMEM((YROWS, YCOLS), F32),
            pltpu.VMEM((YROWS, YCOLS), F32),
            pltpu.VMEM((FF, COLS), F32),
            dma((8,)),
            dma((5,)),
            dma((4,)), dma((4,)),
            dma((NG, 5)), dma((NG, 4)),
            dma((NG, 4)), dma((NG, 4)),
            dma((NG, 4)), dma((NG, 4)),
            dma((4, 2)), dma((4, 2)),
            dma((NG, 3)), dma((NG, 5)),
            dma((8,)), dma((8,)),
            dma((1,)), dma((1,)),
            dma((8,)), dma((8,)),
        ],
        compiler_params=pltpu.CompilerParams(
            collective_id=0, has_side_effects=True, vmem_limit_bytes=54 * 1024 * 1024
        ),
        cost_estimate=pl.CostEstimate(
            flops=11_300_000_000, bytes_accessed=16_000_000, transcendentals=T * FF
        ),
    )(tokens, hidden_grad.T, gate_next, up_next, inner_gate, anchor, momentum)
    return pl.pallas_call(
        results,
        out_shape=shapes,
        in_specs=[pl.BlockSpec(memory_space=pltpu.VMEM)] * 5,
        out_specs=[pl.BlockSpec(memory_space=pl.ANY)] * 5,
        scratch_shapes=[dma((4 + PARTS,))],
        compiler_params=pltpu.CompilerParams(vmem_limit_bytes=16 * 1024 * 1024),
    )(*outs)


def solution(mesh):
    return jax.shard_map(
        shards,
        mesh=mesh,
        in_specs=(
            P(("replica", "fsdp"), None),
            P(("replica", "fsdp"), None),
            P("replica", None, "fsdp"),
            P("replica", None, "fsdp"),
            P("replica", None, "fsdp"),
            P(None, "fsdp"),
            P(None, "fsdp"),
        ),
        out_specs=(
            P(("replica", "fsdp"), None),
            P("replica", None, "fsdp"),
            P("replica", None, "fsdp"),
            P(None, "fsdp"),
            P(None, "fsdp"),
        ),
        check_vma=False,
    )
```

```python
import functools
import jax
import jax.numpy as jnp
from jax import lax
from jax.experimental import pallas as pl
from jax.experimental.pallas import tpu as pltpu
from jax.sharding import PartitionSpec as P

MESH = pl.DeviceIdType.MESH
BF16 = jnp.bfloat16
F32 = jnp.float32

EPS = 1e-06
MU = 0.9
RATE = 0.7

T = 256
FF = 448
COLS = 512
QUART = 2048
D = 8192
RUN = 128

BLOCKS = ((0, 128), (128, 128), (256, 128), (384, 64))
GROUPS = ((0, 256), (256, 512), (512, 768), (768, 896))
ROWS = 896
NG = len(GROUPS)
RING = (False, True, True, True)
YROWS = 224
YCOLS = 128
PARTS = 8


def dot_nt(a, b):
    return lax.dot_general(a, b, (((1,), (1,)), ((), ())), preferred_element_type=F32)


def dot_nn(a, b):
    return lax.dot_general(a, b, (((1,), (0,)), ((), ())), preferred_element_type=F32)


def cots(gate, upval, cotan):
    sig = jax.nn.sigmoid(gate)
    gate_cot = cotan * upval * sig * (1.0 + gate * (1.0 - sig))
    up_cot = cotan * gate * sig
    return gate_cot, up_cot


def kernel(
    tokens, hgrad, gate_n, up_n, inner, anchor, momentum,
    tg_out, gg_out, ug_out, na_out, nm_out,
    xq, w, pst, pown, phop, prx, c, ct, tgs, rsi, rso, hgt, hg,
    inn, anc, mom, dec, yrx, ysum, zrx, tot,
    w_l, in_l, tok_s, tok_r, w_s, w_r, p_s, p_r, c_s, c_r, t_s, t_r, g_s, g_r,
    y_s, y_r, zh_s, zh_r, b_s, b_r, here,
):
    r = lax.axis_index("replica")
    f = lax.axis_index("fsdp")
    x, z = f // 4, f % 4
    zh, y, core = r // 8, (r // 2) % 4, r % 2
    low = z < 2
    end = (z == 0) | (z == 3)
    mid = (z == 1) | (z == 2)
    step = jnp.where(low, 1, -1)
    inward = (r, f + step)
    outward = (r, f - step)

    def xdev(k):
        return (r, ((x + k) % 4) * 4 + z)

    def ydev(dy, dc):
        return (zh * 8 + ((y + dy) % 4) * 2 + (core + dc) % 2, f)

    zpart = ((r + 8) % 16, f)
    ypeers = [(dy, dc) for dy in range(4) for dc in range(2) if (dy, dc) != (0, 0)]

    def colsz(zz):
        return pl.ds(pl.multiple_of(zz * COLS, COLS), COLS)

    def quart(xx):
        return pl.ds(pl.multiple_of(xx * QUART, QUART), QUART)

    barrier = pltpu.get_barrier_semaphore()

    def greet(dev):
        pl.semaphore_signal(barrier, inc=1, device_id=dev, device_id_type=MESH)

    for k in (1, 2, 3):
        greet(xdev(k))
    greet(inward)

    @pl.when(mid)
    def _():
        greet(outward)

    place = r % 8

    def yplace(dy, dc):
        return ((y + dy) % 4) * 2 + (core + dc) % 2

    for dy, dc in ypeers:
        @pl.when(yplace(dy, dc) > place)
        def _():
            greet(ydev(dy, dc))

    @pl.when(zh == 0)
    def _():
        greet(zpart)

    w_local = []
    for b, (u0, n) in enumerate(BLOCKS):
        at = 2 * u0
        w_local.append(pltpu.make_async_copy(
            gate_n.at[0, pl.ds(u0, n)], w.at[pl.ds(at, n), colsz(z)], w_l.at[2 * b]))
        w_local.append(pltpu.make_async_copy(
            up_n.at[0, pl.ds(u0, n)], w.at[pl.ds(at + n, n), colsz(z)], w_l.at[2 * b + 1]))
    for q in w_local:
        q.start()
    own_tok = pltpu.make_async_copy(tokens.at[:, quart(x)], xq.at[0], in_l.at[0])
    in_inner = pltpu.make_async_copy(inner.at[0], inn, in_l.at[1])
    in_anchor = pltpu.make_async_copy(anchor, anc, in_l.at[2])
    in_mom = pltpu.make_async_copy(momentum, mom, in_l.at[3])
    in_hg = pltpu.make_async_copy(hgrad, hgt, in_l.at[4])
    for q in (own_tok, in_inner, in_anchor, in_mom, in_hg):
        q.start()

    pl.semaphore_wait(barrier, 4 + jnp.where(mid, 1, 0) + place + zh)

    def remote(src, dst, ss, rs, dev):
        return pltpu.make_async_remote_copy(
            src_ref=src, dst_ref=dst, send_sem=ss, recv_sem=rs, device_id=dev, device_id_type=MESH)

    tok = {k: remote(tokens.at[:, quart((x + k) % 4)], xq.at[k], tok_s.at[k], tok_r.at[k], xdev(k))
           for k in (1, 2, 3)}
    for k in (2, 1, 3):
        tok[k].start()

    near_end = jnp.where(low, 0, 3)
    far_mid = jnp.where(low, 2, 1)
    far_end = jnp.where(low, 3, 0)

    def wpiece(g, origin, slot, dev):
        a, b = GROUPS[g]
        ref = w.at[pl.ds(a, b - a), colsz(origin)]
        return remote(ref, ref, w_s.at[g, slot], w_r.at[g, origin], dev)

    def w_wait_local(g):
        w_local[2 * g].wait()
        w_local[2 * g + 1].wait()

    def w_start():
        for g in range(NG):
            w_wait_local(g)

            @pl.when(end if g else end | mid)
            def _():
                wpiece(g, z, 0, inward).start()

            if g == 0:
                @pl.when(mid)
                def _():
                    wpiece(g, z, 1, outward).start()

    def w_near(g):
        @pl.when(mid)
        def _():
            wpiece(g, near_end, 2, inward).wait_recv()
            wpiece(g, near_end, 2, inward).start()
            wpiece(g, far_mid, 3, outward).wait_recv()
            wpiece(g, far_mid, 3, outward).start()
            if g + 1 < NG:
                wpiece(g + 1, z, 0, inward).start()
                wpiece(g + 1, z, 1, outward).start()

    def w_far(g):
        @pl.when(mid)
        def _():
            wpiece(g, far_end, 4, outward).wait_recv()
            wpiece(g, far_end, 4, outward).start()

    def w_here(g):
        @pl.when(end)
        def _():
            wpiece(g, z + step, 0, inward).wait_recv()
            wpiece(g, far_mid, 0, inward).wait_recv()
            wpiece(g, far_end, 0, inward).wait_recv()

    def w_drain(g):
        wpiece(g, z, 0, inward).wait_send()

        @pl.when(mid)
        def _():
            wpiece(g, z, 1, outward).wait_send()
            wpiece(g, near_end, 2, inward).wait_send()
            wpiece(g, far_mid, 3, outward).wait_send()
            wpiece(g, far_end, 4, outward).wait_send()

    def yslice(ref, yy, cc):
        return ref.at[pl.ds(pl.multiple_of(cc * YROWS, YROWS), YROWS),
                      pl.ds(pl.multiple_of(yy * YCOLS, YCOLS), YCOLS)]

    def yscatter(i):
        dy, dc = ypeers[i]
        slot = dy * 2 + dc
        return remote(yslice(dec, (y + dy) % 4, (core + dc) % 2), yrx.at[slot],
                      y_s.at[slot], y_r.at[slot], ydev(dy, dc))

    def ygather(i):
        dy, dc = ypeers[i]
        slot = dy * 2 + dc
        return remote(yslice(tot, y, core), yslice(tot, y, core), b_s.at[slot], b_r.at[slot], ydev(dy, dc))

    def ygather_in(i):
        dy, dc = ypeers[i]
        slot = dy * 2 + dc
        ref = yslice(tot, (y + 4 - dy) % 4, (core + dc) % 2)
        return remote(ref, ref, b_s.at[slot], b_r.at[slot], ydev(dy, dc))

    zswap = remote(ysum.at[...], zrx.at[...], zh_s.at[0], zh_r.at[0], zpart)

    def answer(dev):
        pl.semaphore_signal(here, inc=1, device_id=dev, device_id_type=MESH)

    def outer_answer():
        for dy, dc in ypeers:
            @pl.when(yplace(dy, dc) < place)
            def _():
                answer(ydev(dy, dc))

        @pl.when(zh == 1)
        def _():
            answer(zpart)

    def outer_scatter():
        @pl.when(r < 15)
        def _():
            pl.semaphore_wait(here, 8 - place - zh)

        for i in range(7):
            yscatter(i).start()

    def outer_decode():
        in_anchor.wait()
        in_inner.wait()
        for j in range(COLS // RUN):
            s = slice(j * RUN, (j + 1) * RUN)
            delta = anc[:, s] - inn[:, s].astype(F32)
            scale = jnp.max(jnp.abs(delta), axis=-1, keepdims=True) + EPS
            code = jnp.floor((delta / scale) * 7.0 + 0.5)
            dec[:, s] = (scale * code / 7.0).astype(BF16)

    def outer_sum():
        total = yslice(dec, y, core)[...].astype(F32)
        for i in range(7):
            yscatter(i).wait_recv()
        for i in range(7):
            dy, dc = ypeers[i]
            total = total + yrx[dy * 2 + dc].astype(F32)
        ysum[...] = total
        zswap.start()

    def outer_share():
        zswap.wait_recv()
        yslice(tot, y, core)[...] = ysum[...] + zrx[...]
        for i in range(7):
            ygather(i).start()

    def outer_finish():
        in_mom.wait()
        for i in range(7):
            ygather_in(i).wait_recv()
        grad = tot[...] / 16.0
        new_m = MU * mom[...] + grad
        nm_out[...] = new_m
        na_out[...] = anc[...] - RATE * (grad + MU * new_m)

    def lanes(g):
        a, b = GROUPS[g]
        return pl.ds(a, b - a)

    lower, upper = pl.ds(0, T // 2), pl.ds(T // 2, T // 2)

    def hop_copy(g, i):
        rows = (lower, upper)[i]
        return remote(pst.at[2, rows, lanes(g)], phop.at[rows, lanes(g)],
                      p_s.at[g, 2 * i], p_r.at[g, 2 * i], xdev((1, 3)[i]))

    def part_copy(g, k):
        return remote(pst.at[k, :, lanes(g)], prx.at[k // 2, :, lanes(g)], p_s.at[g, k], p_r.at[g, k], xdev(4 - k))

    def cot_copy(g, k):
        return remote(c.at[0, :, lanes(g)], c.at[k, :, lanes(g)], c_s.at[g, k], c_r.at[g, k], xdev(k))

    def cot_hop(g, i):
        rows = (lower, upper)[i]
        return remote(c.at[(1, 3)[i], rows, lanes(g)], c.at[2, rows, lanes(g)],
                      c_s.at[g, 2 * i], c_r.at[g, 2 * i], xdev((1, 3)[i]))

    def part_far(g):
        return remote(pst.at[2, :, lanes(g)], phop.at[:, lanes(g)], p_s.at[g, 0], p_r.at[g, 0], xdev(2))

    def opposite(g):
        a, b = GROUPS[g]
        pst[2, :, a:b] = dot_nt(xq[2], w[a:b, :]).astype(BF16)
        if not RING[g]:
            part_far(g).start()
            return
        for i in range(2):
            hop_copy(g, i).start()

    def neighbours(g):
        a, b = GROUPS[g]
        half = T // 2
        for i, k in enumerate((3, 1)):
            rows = slice(i * half, (i + 1) * half)
            other = slice((1 - i) * half, (2 - i) * half)
            part = dot_nt(xq[k], w[a:b, :])
            if RING[g]:
                hop_copy(g, i).wait_recv()
                pst[k, rows, a:b] = (part[rows] + phop[rows, a:b].astype(F32)).astype(BF16)
                pst[k, other, a:b] = part[other].astype(BF16)
            else:
                pst[k, :, a:b] = part.astype(BF16)
            part_copy(g, k).start()

    def own_part(g):
        a, b = GROUPS[g]
        pown[:, a:b] = dot_nt(xq[0], w[a:b, :])

    def owner(g):
        a, b = GROUPS[g]
        for k in (3, 1):
            part_copy(g, k).wait_recv()
        if not RING[g]:
            part_far(g).wait_recv()
        for u0, n in BLOCKS:
            at = 2 * u0
            if not a <= at < b:
                continue
            full = slice(at, at + 2 * n)
            total = pown[:, full] + prx[0, :, full].astype(F32) + prx[1, :, full].astype(F32)
            if not RING[g]:
                total = total + phop[:, full].astype(F32)
            if n == 128:
                gc, uc = cots(total[:, :n], total[:, n:], hg[:, u0:u0 + n].astype(F32))
                c[0, :, at:at + n] = gc.astype(BF16)
                c[0, :, at + n:at + 2 * n] = uc.astype(BF16)
            else:
                part = hg[:, u0:u0 + n].astype(F32)
                cotan = jnp.concatenate([part, part], axis=1)
                turned = pltpu.roll(total, n, 1)
                first = lax.broadcasted_iota(jnp.int32, total.shape, 1) < n
                gc, uc = cots(jnp.where(first, total, turned), jnp.where(first, turned, total), cotan)
                c[0, :, full] = jnp.where(first, gc, uc).astype(BF16)
        for k in (1, 3) if RING[g] else (2, 1, 3):
            cot_copy(g, k).start()

    def cot_pass(g):
        for i, k in enumerate((1, 3)):
            cot_copy(g, k).wait_recv()
            cot_hop(g, i).start()

    def cot_last(g):
        if not RING[g]:
            cot_copy(g, 2).wait_recv()
            return
        for i in range(2):
            cot_hop(g, i).wait_recv()

    def turn(g):
        a, b = GROUPS[g]
        for k in range(4):
            ct[a:b, k * T:(k + 1) * T] = c[k, :, a:b].T

    def gathered(g):
        a, b = GROUPS[g]
        if not RING[g]:
            for k in (1, 3):
                cot_copy(g, k).wait_recv()
        for k in (0, 1, 3):
            ct[a:b, k * T:(k + 1) * T] = c[k, :, a:b].T
        cot_last(g)
        ct[a:b, 2 * T:3 * T] = c[2, :, a:b].T

    dest_a = jnp.where(low, 3, 0)
    dest_b = jnp.where(low, 2, 1)
    dest_c = jnp.where(z == 0, 1, jnp.where(z == 1, 0, jnp.where(z == 2, 3, 2)))
    dev_c = (r, f + jnp.where(end, step, -step))
    slot_a = jnp.where(end, 0, 3)
    slot_b = jnp.where(end, 1, 4)
    sends = ((dest_a, inward, slot_a, 0), (dest_b, inward, slot_b, 1), (dest_c, dev_c, 2, 3))

    def grad_copy(g, i):
        a, b = GROUPS[g]
        dest, dev, slot, _ = sends[i]
        return remote(rso.at[i, pl.ds(a, b - a)], rsi.at[slot, pl.ds(a, b - a)],
                      g_s.at[g, i], g_r.at[g, slot], dev)

    def grad_in(g, slot):
        a, b = GROUPS[g]
        ref = rsi.at[slot, pl.ds(a, b - a)]
        return remote(ref, ref, g_s.at[g, 0], g_r.at[g, slot], inward)

    def grad_term(g, dest):
        a, b = GROUPS[g]
        return dot_nn(ct[a:b, :], xq[:, :, colsz(dest)].reshape(4 * T, COLS))

    def grad_send(g, i):
        a, b = GROUPS[g]
        dest, _, _, arrives = sends[i]
        rso[i, a:b] = grad_term(g, dest).astype(BF16)

        @pl.when(mid)
        def _():
            grad_in(g, arrives).wait_recv()
            rso[i, a:b] = (rso[i, a:b].astype(F32) + rsi[arrives, a:b].astype(F32)).astype(BF16)

        grad_copy(g, i).start()

    def grad_own(g):
        a, b = GROUPS[g]
        pown2 = grad_term(g, z)
        grad_in(g, 2).wait_recv()
        pown2 = pown2 + rsi[2, a:b].astype(F32)

        @pl.when(mid)
        def _():
            grad_in(g, 4).wait_recv()
            put(g, pown2 + rsi[4, a:b].astype(F32))

        @pl.when(end)
        def _():
            put(g, pown2)

    def put(g, total):
        a, b = GROUPS[g]
        for u0, n in BLOCKS:
            at = 2 * u0 - a
            if 0 <= at < b - a:
                gg_out[0, u0:u0 + n] = total[at:at + n].astype(BF16)
                ug_out[0, u0:u0 + n] = total[at + n:at + 2 * n].astype(BF16)

    def tg_cols(xx, h):
        return pl.ds(pl.multiple_of(xx * QUART + h * (QUART // 2), QUART // 2), QUART // 2)

    def tg_copy(k, h):
        return remote(tgs.at[k, :, pl.ds(h * (QUART // 2), QUART // 2)], tg_out.at[:, tg_cols(x, h)],
                      t_s.at[k, h], t_r.at[k, h], xdev(4 - k))

    def tg_in(k, h):
        return remote(tgs.at[k, :, pl.ds(h * (QUART // 2), QUART // 2)], tg_out.at[:, tg_cols((x + k) % 4, h)],
                      t_s.at[k, h], t_r.at[k, h], xdev(4 - k))

    def token_grad(k, h):
        for j in (2 * h, 2 * h + 1):
            s = slice(j * COLS, (j + 1) * COLS)
            part = dot_nn(c[k], w[:, s]).astype(BF16)
            if k:
                tgs[k, :, s] = part
            else:
                tg_out[:, pl.ds(pl.multiple_of(x * QUART + j * COLS, COLS), COLS)] = part
        if k:
            tg_copy(k, h).start()

    w_start()
    outer_answer()
    outer_decode()
    w_near(0)
    in_hg.wait()
    hg[...] = hgt[...].T
    w_far(0)
    w_near(1)
    outer_scatter()
    own_tok.wait()
    w_here(0)
    tok[2].wait_recv()
    opposite(0)
    w_far(1)
    own_part(0)
    w_near(2)
    w_far(2)
    outer_sum()
    w_near(3)
    w_here(1)
    own_part(1)
    w_far(3)
    tok[1].wait_recv()
    tok[3].wait_recv()
    neighbours(0)
    opposite(1)
    owner(0)
    neighbours(1)
    w_here(2)
    opposite(2)
    own_part(2)
    gathered(0)
    for i in range(3):
        @pl.when(end)
        def _():
            grad_send(0, i)
    w_here(3)
    opposite(3)
    own_part(3)
    outer_share()
    owner(1)
    neighbours(2)
    neighbours(3)
    cot_pass(1)
    owner(2)
    owner(3)
    gathered(1)
    for i in range(3):
        @pl.when(end)
        def _():
            grad_send(1, i)
    for i in range(2):
        @pl.when(mid)
        def _():
            grad_send(0, i)
    cot_pass(2)
    cot_pass(3)
    cot_last(2)
    token_grad(1, 0)
    token_grad(3, 0)
    cot_last(3)
    for k, h in ((2, 0), (2, 1), (1, 1), (3, 1)):
        token_grad(k, h)
    turn(2)
    turn(3)

    @pl.when(mid)
    def _():
        grad_send(0, 2)
    for i in range(3):
        @pl.when(mid)
        def _():
            grad_send(1, i)
    for i in range(3):
        grad_send(2, i)
    for i in range(3):
        grad_send(3, i)
    token_grad(0, 0)
    token_grad(0, 1)
    outer_finish()
    for g in range(4):
        grad_own(g)

    for k in (1, 3, 2):
        for h in range(2):
            tg_in(k, h).wait_recv()
    for k in (1, 2, 3):
        tok[k].wait_send()
        for h in range(2):
            tg_copy(k, h).wait_send()
        for g in range(NG):
            if k != 2:
                part_copy(g, k).wait_send()
                cot_copy(g, k).wait_send()
    for g in range(NG):
        w_drain(g)
        if RING[g]:
            for i in range(2):
                hop_copy(g, i).wait_send()
                cot_hop(g, i).wait_send()
        else:
            part_far(g).wait_send()
            cot_copy(g, 2).wait_send()
        for i in range(3):
            grad_copy(g, i).wait_send()
    for i in range(7):
        yscatter(i).wait_send()
        ygather(i).wait_send()
    zswap.wait_send()


def results(tg, gg, ug, na, nm, tg_out, gg_out, ug_out, na_out, nm_out, out_s):
    ways = [(na, na_out), (nm, nm_out), (gg, gg_out), (ug, ug_out)]
    for i in range(PARTS):
        rows = pl.ds(i * (T // PARTS), T // PARTS)
        ways.append((tg.at[rows], tg_out.at[rows]))
    outs = [pltpu.make_async_copy(src, dst, out_s.at[i]) for i, (src, dst) in enumerate(ways)]
    for o in outs:
        o.start()
    for o in outs:
        o.wait()


def shards(tokens, hidden_grad, gate_next, up_next, inner_gate, anchor, momentum):
    dma = pltpu.SemaphoreType.DMA
    shapes = (
        jax.ShapeDtypeStruct((T, D), BF16),
        jax.ShapeDtypeStruct((1, FF, COLS), BF16),
        jax.ShapeDtypeStruct((1, FF, COLS), BF16),
        jax.ShapeDtypeStruct((FF, COLS), F32),
        jax.ShapeDtypeStruct((FF, COLS), F32),
    )
    outs = pl.pallas_call(
        kernel,
        out_shape=tuple(pltpu.VMEM(o.shape, o.dtype) for o in shapes),
        in_specs=[pl.BlockSpec(memory_space=pltpu.HBM)] * 7,
        out_specs=[pl.BlockSpec(memory_space=pltpu.VMEM)] * 5,
        scratch_shapes=[
            pltpu.VMEM((4, T, QUART), BF16),
            pltpu.VMEM((ROWS, QUART), BF16),
            pltpu.VMEM((4, T, ROWS), BF16),
            pltpu.VMEM((T, ROWS), F32),
            pltpu.VMEM((T, ROWS), BF16),
            pltpu.VMEM((2, T, ROWS), BF16),
            pltpu.VMEM((4, T, ROWS), BF16),
            pltpu.VMEM((ROWS, 4 * T), BF16),
            pltpu.VMEM((4, T, QUART), BF16),
            pltpu.VMEM((5, ROWS, COLS), BF16),
            pltpu.VMEM((3, ROWS, COLS), BF16),
            pltpu.VMEM((FF, T), BF16),
            pltpu.VMEM((T, FF), BF16),
            pltpu.VMEM((FF, COLS), BF16),
            pltpu.VMEM((FF, COLS), F32),
            pltpu.VMEM((FF, COLS), F32),
            pltpu.VMEM((FF, COLS), BF16),
            pltpu.VMEM((8, YROWS, YCOLS), BF16),
            pltpu.VMEM((YROWS, YCOLS), F32),
            pltpu.VMEM((YROWS, YCOLS), F32),
            pltpu.VMEM((FF, COLS), F32),
            dma((8,)),
            dma((5,)),
            dma((4,)), dma((4,)),
            dma((NG, 5)), dma((NG, 4)),
            dma((NG, 4)), dma((NG, 4)),
            dma((NG, 4)), dma((NG, 4)),
            dma((4, 2)), dma((4, 2)),
            dma((NG, 3)), dma((NG, 5)),
            dma((8,)), dma((8,)),
            dma((1,)), dma((1,)),
            dma((8,)), dma((8,)),
            pltpu.SemaphoreType.REGULAR,
        ],
        compiler_params=pltpu.CompilerParams(
            collective_id=0, has_side_effects=True, vmem_limit_bytes=54 * 1024 * 1024
        ),
        cost_estimate=pl.CostEstimate(
            flops=11_300_000_000, bytes_accessed=16_000_000, transcendentals=T * FF
        ),
    )(tokens, hidden_grad.T, gate_next, up_next, inner_gate, anchor, momentum)
    return pl.pallas_call(
        results,
        out_shape=shapes,
        in_specs=[pl.BlockSpec(memory_space=pltpu.VMEM)] * 5,
        out_specs=[pl.BlockSpec(memory_space=pl.ANY)] * 5,
        scratch_shapes=[dma((4 + PARTS,))],
        compiler_params=pltpu.CompilerParams(vmem_limit_bytes=16 * 1024 * 1024),
    )(*outs)


def solution(mesh):
    return jax.shard_map(
        shards,
        mesh=mesh,
        in_specs=(
            P(("replica", "fsdp"), None),
            P(("replica", "fsdp"), None),
            P("replica", None, "fsdp"),
            P("replica", None, "fsdp"),
            P("replica", None, "fsdp"),
            P(None, "fsdp"),
            P(None, "fsdp"),
        ),
        out_specs=(
            P(("replica", "fsdp"), None),
            P("replica", None, "fsdp"),
            P("replica", None, "fsdp"),
            P(None, "fsdp"),
            P(None, "fsdp"),
        ),
        check_vma=False,
    )
```

```python
import functools
import jax
import jax.numpy as jnp
from jax import lax
from jax.experimental import pallas as pl
from jax.experimental.pallas import tpu as pltpu
from jax.sharding import PartitionSpec as P

MESH = pl.DeviceIdType.MESH
BF16 = jnp.bfloat16
F32 = jnp.float32

EPS = 1e-06
MU = 0.9
RATE = 0.7

T = 256
FF = 448
COLS = 512
QUART = 2048
D = 8192
RUN = 128

BLOCKS = ((0, 128), (128, 128), (256, 128), (384, 64))
GROUPS = ((0, 256), (256, 512), (512, 768), (768, 896))
ROWS = 896
NG = len(GROUPS)
RING = (False, True, True, True)
YROWS = 224
YCOLS = 128
PARTS = 8


def dot_nt(a, b):
    return lax.dot_general(a, b, (((1,), (1,)), ((), ())), preferred_element_type=F32)


def dot_nn(a, b):
    return lax.dot_general(a, b, (((1,), (0,)), ((), ())), preferred_element_type=F32)


def cots(gate, upval, cotan):
    sig = jax.nn.sigmoid(gate)
    gate_cot = cotan * upval * sig * (1.0 + gate * (1.0 - sig))
    up_cot = cotan * gate * sig
    return gate_cot, up_cot


def kernel(
    tokens, hgrad, gate_n, up_n, inner, anchor, momentum,
    tg_out, gg_out, ug_out, na_out, nm_out,
    xq, w, pst, pown, phop, prx, c, ct, tgs, rsi, rso, hgt, hg,
    inn, anc, mom, dec, yrx, ysum, zrx, tot,
    w_l, in_l, tok_s, tok_r, w_s, w_r, p_s, p_r, c_s, c_r, t_s, t_r, g_s, g_r,
    y_s, y_r, zh_s, zh_r, b_s, b_r, here,
):
    r = lax.axis_index("replica")
    f = lax.axis_index("fsdp")
    x, z = f // 4, f % 4
    zh, y, core = r // 8, (r // 2) % 4, r % 2
    low = z < 2
    end = (z == 0) | (z == 3)
    mid = (z == 1) | (z == 2)
    step = jnp.where(low, 1, -1)
    inward = (r, f + step)
    outward = (r, f - step)

    def xdev(k):
        return (r, ((x + k) % 4) * 4 + z)

    def ydev(dy, dc):
        return (zh * 8 + ((y + dy) % 4) * 2 + (core + dc) % 2, f)

    zpart = ((r + 8) % 16, f)
    ypeers = [(dy, dc) for dy in range(4) for dc in range(2) if (dy, dc) != (0, 0)]

    def colsz(zz):
        return pl.ds(pl.multiple_of(zz * COLS, COLS), COLS)

    def quart(xx):
        return pl.ds(pl.multiple_of(xx * QUART, QUART), QUART)

    barrier = pltpu.get_barrier_semaphore()

    def greet(dev):
        pl.semaphore_signal(barrier, inc=1, device_id=dev, device_id_type=MESH)

    for k in (1, 2, 3):
        greet(xdev(k))
    greet(inward)

    @pl.when(mid)
    def _():
        greet(outward)

    place = r % 8

    def yplace(dy, dc):
        return ((y + dy) % 4) * 2 + (core + dc) % 2

    for dy, dc in ypeers:
        @pl.when(yplace(dy, dc) > place)
        def _():
            greet(ydev(dy, dc))

    @pl.when(zh == 0)
    def _():
        greet(zpart)

    w_local = []
    for b, (u0, n) in enumerate(BLOCKS):
        at = 2 * u0
        w_local.append(pltpu.make_async_copy(
            gate_n.at[0, pl.ds(u0, n)], w.at[pl.ds(at, n), colsz(z)], w_l.at[2 * b]))
        w_local.append(pltpu.make_async_copy(
            up_n.at[0, pl.ds(u0, n)], w.at[pl.ds(at + n, n), colsz(z)], w_l.at[2 * b + 1]))
    for q in w_local:
        q.start()
    own_tok = pltpu.make_async_copy(tokens.at[:, quart(x)], xq.at[0], in_l.at[0])
    in_inner = pltpu.make_async_copy(inner.at[0], inn, in_l.at[1])
    in_anchor = pltpu.make_async_copy(anchor, anc, in_l.at[2])
    in_mom = pltpu.make_async_copy(momentum, mom, in_l.at[3])
    in_hg = pltpu.make_async_copy(hgrad, hgt, in_l.at[4])
    for q in (own_tok, in_inner, in_anchor, in_mom, in_hg):
        q.start()

    pl.semaphore_wait(barrier, 4 + jnp.where(mid, 1, 0) + place + zh)

    def remote(src, dst, ss, rs, dev):
        return pltpu.make_async_remote_copy(
            src_ref=src, dst_ref=dst, send_sem=ss, recv_sem=rs, device_id=dev, device_id_type=MESH)

    tok = {k: remote(tokens.at[:, quart((x + k) % 4)], xq.at[k], tok_s.at[k], tok_r.at[k], xdev(k))
           for k in (1, 2, 3)}
    for k in (2, 1, 3):
        tok[k].start()

    near_end = jnp.where(low, 0, 3)
    far_mid = jnp.where(low, 2, 1)
    far_end = jnp.where(low, 3, 0)

    def wpiece(g, origin, slot, dev):
        a, b = GROUPS[g]
        ref = w.at[pl.ds(a, b - a), colsz(origin)]
        return remote(ref, ref, w_s.at[g, slot], w_r.at[g, origin], dev)

    def w_wait_local(g):
        w_local[2 * g].wait()
        w_local[2 * g + 1].wait()

    def w_start():
        for g in range(NG):
            w_wait_local(g)

            @pl.when(end if g else end | mid)
            def _():
                wpiece(g, z, 0, inward).start()

            if g == 0:
                @pl.when(mid)
                def _():
                    wpiece(g, z, 1, outward).start()

    def w_near(g):
        @pl.when(mid)
        def _():
            wpiece(g, near_end, 2, inward).wait_recv()
            wpiece(g, near_end, 2, inward).start()
            wpiece(g, far_mid, 3, outward).wait_recv()
            wpiece(g, far_mid, 3, outward).start()
            if g + 1 < NG:
                wpiece(g + 1, z, 0, inward).start()
                wpiece(g + 1, z, 1, outward).start()

    def w_far(g):
        @pl.when(mid)
        def _():
            wpiece(g, far_end, 4, outward).wait_recv()
            wpiece(g, far_end, 4, outward).start()

    def w_here(g):
        @pl.when(end)
        def _():
            wpiece(g, z + step, 0, inward).wait_recv()
            wpiece(g, far_mid, 0, inward).wait_recv()
            wpiece(g, far_end, 0, inward).wait_recv()

    def w_drain(g):
        wpiece(g, z, 0, inward).wait_send()

        @pl.when(mid)
        def _():
            wpiece(g, z, 1, outward).wait_send()
            wpiece(g, near_end, 2, inward).wait_send()
            wpiece(g, far_mid, 3, outward).wait_send()
            wpiece(g, far_end, 4, outward).wait_send()

    def yslice(ref, yy, cc):
        return ref.at[pl.ds(pl.multiple_of(cc * YROWS, YROWS), YROWS),
                      pl.ds(pl.multiple_of(yy * YCOLS, YCOLS), YCOLS)]

    def yscatter(i):
        dy, dc = ypeers[i]
        slot = dy * 2 + dc
        return remote(yslice(dec, (y + dy) % 4, (core + dc) % 2), yrx.at[slot],
                      y_s.at[slot], y_r.at[slot], ydev(dy, dc))

    def ygather(i):
        dy, dc = ypeers[i]
        slot = dy * 2 + dc
        return remote(yslice(tot, y, core), yslice(tot, y, core), b_s.at[slot], b_r.at[slot], ydev(dy, dc))

    def ygather_in(i):
        dy, dc = ypeers[i]
        slot = dy * 2 + dc
        ref = yslice(tot, (y + 4 - dy) % 4, (core + dc) % 2)
        return remote(ref, ref, b_s.at[slot], b_r.at[slot], ydev(dy, dc))

    zswap = remote(ysum.at[...], zrx.at[...], zh_s.at[0], zh_r.at[0], zpart)

    def answer(dev):
        pl.semaphore_signal(here, inc=1, device_id=dev, device_id_type=MESH)

    def outer_answer():
        for dy, dc in ypeers:
            @pl.when(yplace(dy, dc) < place)
            def _():
                answer(ydev(dy, dc))

        @pl.when(zh == 1)
        def _():
            answer(zpart)

    def outer_scatter():
        @pl.when(r < 15)
        def _():
            pl.semaphore_wait(here, 8 - place - zh)

        for i in range(7):
            yscatter(i).start()

    def outer_decode():
        in_anchor.wait()
        in_inner.wait()
        for j in range(COLS // RUN):
            s = slice(j * RUN, (j + 1) * RUN)
            delta = anc[:, s] - inn[:, s].astype(F32)
            scale = jnp.max(jnp.abs(delta), axis=-1, keepdims=True) + EPS
            code = jnp.floor((delta / scale) * 7.0 + 0.5)
            dec[:, s] = (scale * code / 7.0).astype(BF16)

    def outer_sum():
        total = yslice(dec, y, core)[...].astype(F32)
        for i in range(7):
            yscatter(i).wait_recv()
        for i in range(7):
            dy, dc = ypeers[i]
            total = total + yrx[dy * 2 + dc].astype(F32)
        ysum[...] = total
        zswap.start()

    def outer_share():
        zswap.wait_recv()
        yslice(tot, y, core)[...] = ysum[...] + zrx[...]
        for i in range(7):
            ygather(i).start()

    def outer_finish():
        in_mom.wait()
        for i in range(7):
            ygather_in(i).wait_recv()
        grad = tot[...] / 16.0
        new_m = MU * mom[...] + grad
        nm_out[...] = new_m
        na_out[...] = anc[...] - RATE * (grad + MU * new_m)

    def lanes(g):
        a, b = GROUPS[g]
        return pl.ds(a, b - a)

    lower, upper = pl.ds(0, T // 2), pl.ds(T // 2, T // 2)

    def hop_copy(g, i):
        rows = (lower, upper)[i]
        return remote(pst.at[2, rows, lanes(g)], phop.at[rows, lanes(g)],
                      p_s.at[g, 2 * i], p_r.at[g, 2 * i], xdev((1, 3)[i]))

    def part_copy(g, k):
        return remote(pst.at[k, :, lanes(g)], prx.at[k // 2, :, lanes(g)], p_s.at[g, k], p_r.at[g, k], xdev(4 - k))

    def cot_copy(g, k):
        return remote(c.at[0, :, lanes(g)], c.at[k, :, lanes(g)], c_s.at[g, k], c_r.at[g, k], xdev(k))

    def cot_hop(g, i):
        rows = (lower, upper)[i]
        return remote(c.at[(1, 3)[i], rows, lanes(g)], c.at[2, rows, lanes(g)],
                      c_s.at[g, 2 * i], c_r.at[g, 2 * i], xdev((1, 3)[i]))

    def part_far(g):
        return remote(pst.at[2, :, lanes(g)], phop.at[:, lanes(g)], p_s.at[g, 0], p_r.at[g, 0], xdev(2))

    def opposite(g):
        a, b = GROUPS[g]
        pst[2, :, a:b] = dot_nt(xq[2], w[a:b, :]).astype(BF16)
        if not RING[g]:
            part_far(g).start()
            return
        for i in range(2):
            hop_copy(g, i).start()

    def neighbours(g):
        a, b = GROUPS[g]
        half = T // 2
        for i, k in enumerate((3, 1)):
            rows = slice(i * half, (i + 1) * half)
            other = slice((1 - i) * half, (2 - i) * half)
            part = dot_nt(xq[k], w[a:b, :])
            if RING[g]:
                hop_copy(g, i).wait_recv()
                pst[k, rows, a:b] = (part[rows] + phop[rows, a:b].astype(F32)).astype(BF16)
                pst[k, other, a:b] = part[other].astype(BF16)
            else:
                pst[k, :, a:b] = part.astype(BF16)
            part_copy(g, k).start()

    def own_part(g):
        a, b = GROUPS[g]
        pown[:, a:b] = dot_nt(xq[0], w[a:b, :])

    def owner(g):
        a, b = GROUPS[g]
        for k in (3, 1):
            part_copy(g, k).wait_recv()
        if not RING[g]:
            part_far(g).wait_recv()
        for u0, n in BLOCKS:
            at = 2 * u0
            if not a <= at < b:
                continue
            full = slice(at, at + 2 * n)
            total = pown[:, full] + prx[0, :, full].astype(F32) + prx[1, :, full].astype(F32)
            if not RING[g]:
                total = total + phop[:, full].astype(F32)
            if n == 128:
                gc, uc = cots(total[:, :n], total[:, n:], hg[:, u0:u0 + n].astype(F32))
                c[0, :, at:at + n] = gc.astype(BF16)
                c[0, :, at + n:at + 2 * n] = uc.astype(BF16)
            else:
                part = hg[:, u0:u0 + n].astype(F32)
                cotan = jnp.concatenate([part, part], axis=1)
                turned = pltpu.roll(total, n, 1)
                first = lax.broadcasted_iota(jnp.int32, total.shape, 1) < n
                gc, uc = cots(jnp.where(first, total, turned), jnp.where(first, turned, total), cotan)
                c[0, :, full] = jnp.where(first, gc, uc).astype(BF16)
        for k in (1, 3) if RING[g] else (2, 1, 3):
            cot_copy(g, k).start()

    def cot_pass(g):
        for i, k in enumerate((1, 3)):
            cot_copy(g, k).wait_recv()
            cot_hop(g, i).start()

    def cot_last(g):
        if not RING[g]:
            cot_copy(g, 2).wait_recv()
            return
        for i in range(2):
            cot_hop(g, i).wait_recv()

    def turn(g):
        a, b = GROUPS[g]
        for k in range(4):
            ct[a:b, k * T:(k + 1) * T] = c[k, :, a:b].T

    def gathered(g):
        a, b = GROUPS[g]
        if not RING[g]:
            for k in (1, 3):
                cot_copy(g, k).wait_recv()
        for k in (0, 1, 3):
            ct[a:b, k * T:(k + 1) * T] = c[k, :, a:b].T
        cot_last(g)
        ct[a:b, 2 * T:3 * T] = c[2, :, a:b].T

    dest_a = jnp.where(low, 3, 0)
    dest_b = jnp.where(low, 2, 1)
    dest_c = jnp.where(z == 0, 1, jnp.where(z == 1, 0, jnp.where(z == 2, 3, 2)))
    dev_c = (r, f + jnp.where(end, step, -step))
    slot_a = jnp.where(end, 0, 3)
    slot_b = jnp.where(end, 1, 4)
    sends = ((dest_a, inward, slot_a, 0), (dest_b, inward, slot_b, 1), (dest_c, dev_c, 2, 3))

    def grad_copy(g, i):
        a, b = GROUPS[g]
        dest, dev, slot, _ = sends[i]
        return remote(rso.at[i, pl.ds(a, b - a)], rsi.at[slot, pl.ds(a, b - a)],
                      g_s.at[g, i], g_r.at[g, slot], dev)

    def grad_in(g, slot):
        a, b = GROUPS[g]
        ref = rsi.at[slot, pl.ds(a, b - a)]
        return remote(ref, ref, g_s.at[g, 0], g_r.at[g, slot], inward)

    def grad_term(g, dest):
        a, b = GROUPS[g]
        return dot_nn(ct[a:b, :], xq[:, :, colsz(dest)].reshape(4 * T, COLS))

    def grad_send(g, i):
        a, b = GROUPS[g]
        dest, _, _, arrives = sends[i]
        rso[i, a:b] = grad_term(g, dest).astype(BF16)

        @pl.when(mid)
        def _():
            grad_in(g, arrives).wait_recv()
            rso[i, a:b] = (rso[i, a:b].astype(F32) + rsi[arrives, a:b].astype(F32)).astype(BF16)

        grad_copy(g, i).start()

    def grad_own(g):
        a, b = GROUPS[g]
        pown2 = grad_term(g, z)
        grad_in(g, 2).wait_recv()
        pown2 = pown2 + rsi[2, a:b].astype(F32)

        @pl.when(mid)
        def _():
            grad_in(g, 4).wait_recv()
            put(g, pown2 + rsi[4, a:b].astype(F32))

        @pl.when(end)
        def _():
            put(g, pown2)

    def put(g, total):
        a, b = GROUPS[g]
        for u0, n in BLOCKS:
            at = 2 * u0 - a
            if 0 <= at < b - a:
                gg_out[0, u0:u0 + n] = total[at:at + n].astype(BF16)
                ug_out[0, u0:u0 + n] = total[at + n:at + 2 * n].astype(BF16)

    def tg_cols(xx, h):
        return pl.ds(pl.multiple_of(xx * QUART + h * (QUART // 2), QUART // 2), QUART // 2)

    def tg_copy(k, h):
        return remote(tgs.at[k, :, pl.ds(h * (QUART // 2), QUART // 2)], tg_out.at[:, tg_cols(x, h)],
                      t_s.at[k, h], t_r.at[k, h], xdev(4 - k))

    def tg_in(k, h):
        return remote(tgs.at[k, :, pl.ds(h * (QUART // 2), QUART // 2)], tg_out.at[:, tg_cols((x + k) % 4, h)],
                      t_s.at[k, h], t_r.at[k, h], xdev(4 - k))

    def token_grad(k, h):
        for j in (2 * h, 2 * h + 1):
            s = slice(j * COLS, (j + 1) * COLS)
            part = dot_nn(c[k], w[:, s]).astype(BF16)
            if k:
                tgs[k, :, s] = part
            else:
                tg_out[:, pl.ds(pl.multiple_of(x * QUART + j * COLS, COLS), COLS)] = part
        if k:
            tg_copy(k, h).start()

    w_start()
    outer_answer()
    outer_decode()
    w_near(0)
    in_hg.wait()
    hg[...] = hgt[...].T
    w_far(0)
    w_near(1)
    outer_scatter()
    own_tok.wait()
    w_here(0)
    tok[2].wait_recv()
    opposite(0)
    w_far(1)
    own_part(0)
    w_near(2)
    w_far(2)
    outer_sum()
    w_near(3)
    w_here(1)
    own_part(1)
    w_far(3)
    tok[1].wait_recv()
    tok[3].wait_recv()
    neighbours(0)
    opposite(1)
    owner(0)
    neighbours(1)
    w_here(2)
    opposite(2)
    own_part(2)
    gathered(0)
    for i in range(3):
        @pl.when(end)
        def _():
            grad_send(0, i)
    w_here(3)
    opposite(3)
    own_part(3)
    outer_share()
    owner(1)
    neighbours(2)
    neighbours(3)
    cot_pass(1)
    owner(2)
    owner(3)
    gathered(1)
    for i in range(3):
        @pl.when(end)
        def _():
            grad_send(1, i)
    for i in range(2):
        @pl.when(mid)
        def _():
            grad_send(0, i)
    cot_pass(2)
    cot_pass(3)
    cot_last(2)
    token_grad(1, 0)
    token_grad(3, 0)
    cot_last(3)
    for k, h in ((2, 0), (2, 1), (1, 1), (3, 1)):
        token_grad(k, h)
    turn(2)
    turn(3)

    @pl.when(mid)
    def _():
        grad_send(0, 2)
    for i in range(3):
        @pl.when(mid)
        def _():
            grad_send(1, i)
    token_grad(0, 0)
    token_grad(0, 1)
    outer_finish()
    for i in range(3):
        grad_send(2, i)
    grad_own(0)
    grad_own(1)
    for i in range(3):
        grad_send(3, i)
    grad_own(2)
    grad_own(3)

    for k in (1, 3, 2):
        for h in range(2):
            tg_in(k, h).wait_recv()
    for k in (1, 2, 3):
        tok[k].wait_send()
        for h in range(2):
            tg_copy(k, h).wait_send()
        for g in range(NG):
            if k != 2:
                part_copy(g, k).wait_send()
                cot_copy(g, k).wait_send()
    for g in range(NG):
        w_drain(g)
        if RING[g]:
            for i in range(2):
                hop_copy(g, i).wait_send()
                cot_hop(g, i).wait_send()
        else:
            part_far(g).wait_send()
            cot_copy(g, 2).wait_send()
        for i in range(3):
            grad_copy(g, i).wait_send()
    for i in range(7):
        yscatter(i).wait_send()
        ygather(i).wait_send()
    zswap.wait_send()


def results(tg, gg, ug, na, nm, tg_out, gg_out, ug_out, na_out, nm_out, out_s):
    ways = [(na, na_out), (nm, nm_out), (gg, gg_out), (ug, ug_out)]
    for i in range(PARTS):
        rows = pl.ds(i * (T // PARTS), T // PARTS)
        ways.append((tg.at[rows], tg_out.at[rows]))
    outs = [pltpu.make_async_copy(src, dst, out_s.at[i]) for i, (src, dst) in enumerate(ways)]
    for o in outs:
        o.start()
    for o in outs:
        o.wait()


def shards(tokens, hidden_grad, gate_next, up_next, inner_gate, anchor, momentum):
    dma = pltpu.SemaphoreType.DMA
    shapes = (
        jax.ShapeDtypeStruct((T, D), BF16),
        jax.ShapeDtypeStruct((1, FF, COLS), BF16),
        jax.ShapeDtypeStruct((1, FF, COLS), BF16),
        jax.ShapeDtypeStruct((FF, COLS), F32),
        jax.ShapeDtypeStruct((FF, COLS), F32),
    )
    outs = pl.pallas_call(
        kernel,
        out_shape=tuple(pltpu.VMEM(o.shape, o.dtype) for o in shapes),
        in_specs=[pl.BlockSpec(memory_space=pltpu.HBM)] * 7,
        out_specs=[pl.BlockSpec(memory_space=pltpu.VMEM)] * 5,
        scratch_shapes=[
            pltpu.VMEM((4, T, QUART), BF16),
            pltpu.VMEM((ROWS, QUART), BF16),
            pltpu.VMEM((4, T, ROWS), BF16),
            pltpu.VMEM((T, ROWS), F32),
            pltpu.VMEM((T, ROWS), BF16),
            pltpu.VMEM((2, T, ROWS), BF16),
            pltpu.VMEM((4, T, ROWS), BF16),
            pltpu.VMEM((ROWS, 4 * T), BF16),
            pltpu.VMEM((4, T, QUART), BF16),
            pltpu.VMEM((5, ROWS, COLS), BF16),
            pltpu.VMEM((3, ROWS, COLS), BF16),
            pltpu.VMEM((FF, T), BF16),
            pltpu.VMEM((T, FF), BF16),
            pltpu.VMEM((FF, COLS), BF16),
            pltpu.VMEM((FF, COLS), F32),
            pltpu.VMEM((FF, COLS), F32),
            pltpu.VMEM((FF, COLS), BF16),
            pltpu.VMEM((8, YROWS, YCOLS), BF16),
            pltpu.VMEM((YROWS, YCOLS), F32),
            pltpu.VMEM((YROWS, YCOLS), F32),
            pltpu.VMEM((FF, COLS), F32),
            dma((8,)),
            dma((5,)),
            dma((4,)), dma((4,)),
            dma((NG, 5)), dma((NG, 4)),
            dma((NG, 4)), dma((NG, 4)),
            dma((NG, 4)), dma((NG, 4)),
            dma((4, 2)), dma((4, 2)),
            dma((NG, 3)), dma((NG, 5)),
            dma((8,)), dma((8,)),
            dma((1,)), dma((1,)),
            dma((8,)), dma((8,)),
            pltpu.SemaphoreType.REGULAR,
        ],
        compiler_params=pltpu.CompilerParams(
            collective_id=0, has_side_effects=True, vmem_limit_bytes=54 * 1024 * 1024
        ),
        cost_estimate=pl.CostEstimate(
            flops=11_300_000_000, bytes_accessed=16_000_000, transcendentals=T * FF
        ),
    )(tokens, hidden_grad.T, gate_next, up_next, inner_gate, anchor, momentum)
    return pl.pallas_call(
        results,
        out_shape=shapes,
        in_specs=[pl.BlockSpec(memory_space=pltpu.VMEM)] * 5,
        out_specs=[pl.BlockSpec(memory_space=pl.ANY)] * 5,
        scratch_shapes=[dma((4 + PARTS,))],
        compiler_params=pltpu.CompilerParams(vmem_limit_bytes=16 * 1024 * 1024),
    )(*outs)


def solution(mesh):
    return jax.shard_map(
        shards,
        mesh=mesh,
        in_specs=(
            P(("replica", "fsdp"), None),
            P(("replica", "fsdp"), None),
            P("replica", None, "fsdp"),
            P("replica", None, "fsdp"),
            P("replica", None, "fsdp"),
            P(None, "fsdp"),
            P(None, "fsdp"),
        ),
        out_specs=(
            P(("replica", "fsdp"), None),
            P("replica", None, "fsdp"),
            P("replica", None, "fsdp"),
            P(None, "fsdp"),
            P(None, "fsdp"),
        ),
        check_vma=False,
    )
```
